32 devices in a mesh: ka: 4 (over y, x), band: 8 (over z, core).
Axes of the slice: x: 2, y: 2, z: 4, core: 2. Of those that a mesh axis runs over, the one named last changes fastest.
Arguments:
- targets: float32 [32, 2, 24, 576], P(('ka', 'band')), may hold values from -6 to 6
- occupied: bfloat16 [32, 2, 24, 576], P(('ka', 'band')), may hold values from -3 to 3
- kernels: float32 [16, 24, 576], replicated, may hold values from 0.1 to 2
- partner: int32 [4], replicated, may hold values from 0 to 3, as said below
- kernel_index: int32 [8, 8], replicated, may hold values from 0 to 15
Outputs:
- exchange: float32 [32, 2, 24, 576], P(('ka', 'band'))
The draws below stay inside these ranges and needn't reach their ends.
Inputs may be any that keep to these rules, and one draw needn't show every extreme that they name: partner is a permutation of the groups.
All inputs are finite; a program needn't handle non-finite values.
Results may differ from the reference program's by a relative error of at most 0.0003.
Values may be sent and summed in bfloat16 or wider, within the bound.
No kernel may reach another device: no remote copies, remote signals or barrier semaphores. Data moves between devices by JAX's collectives and lax.ppermute only.
A program may use at most 64 MiB of HBM per device.

```python
import math
import jax
import jax.numpy as jnp
from jax import lax

GRID = 24
KPT_DEV = 2
NKERN = 16
NKPT = 8
NOCC_K = 4
NTGT_K = 4
N_KA = 4
N_BAND = 8


def draw_partner(key, part):
    first_key = jax.random.fold_in(key, 11)
    second_key = jax.random.fold_in(key, 23)
    order = jax.random.permutation(first_key, N_KA).astype(jnp.int32)
    chosen = jax.random.randint(second_key, (), 0, N_KA).astype(jnp.int32)
    wanted = (chosen + N_KA // 2) % N_KA
    holder = jnp.argmax(order == wanted).astype(jnp.int32)
    previous = order[chosen]
    order = order.at[holder].set(previous)
    order = order.at[chosen].set(wanted)
    return order.astype(jnp.int32)


def set_ends(drawn, rng, smallest, largest):
    shape = drawn.shape
    place = [jax.random.randint(jax.random.fold_in(rng, axis), (), 0, shape[axis]) for axis in range(len(shape))]
    drawn = drawn.at[tuple(place)].set(smallest)
    longest = shape.index(max(shape))
    place[longest] = (place[longest] + 1) % shape[longest]
    return drawn.at[tuple(place)].set(largest)


def block_scale(stream_key, dims, shards, least, largest):
    level = 1.0
    for position, shards_of in shards:
        draws = jax.random.uniform(jax.random.fold_in(jax.random.fold_in(stream_key, 6), position), (shards_of,), jnp.float32, least / len(shards), largest / len(shards))
        level = level * jnp.repeat(jnp.exp(draws), dims[position] // shards_of).reshape((-1,) + (1,) * (len(dims) - 1 - position))
    return level


def gaussian(rng, shape, width, most, cuts=(), kind=jnp.bfloat16):
    values = jax.random.normal(rng, shape, jnp.float32) * width
    if len(cuts) > 0:
        values = block_scale(rng, shape, cuts, -0.22, 0.18) * values
    return jnp.clip(values, min=-most, max=most).astype(kind)


def setup_inputs(seed: int = 0) -> dict:
    splits = jax.random.split(jax.random.key(seed), 6)
    return {
        "targets": gaussian(splits[0], (NKPT * NTGT_K, 2, GRID, GRID * GRID), 1.0, 6.0, ((0, 32),), jnp.float32),
        "occupied": gaussian(splits[1], (NKPT * NOCC_K, 2, GRID, GRID * GRID), 0.5, 3.0, ((0, 32),)),
        "kernels": jnp.clip(jnp.exp(jax.random.uniform(splits[2], (NKERN, GRID, GRID * GRID), jnp.float32, math.log(0.1), math.log(2.0))), 0.1, 2.0),
        "partner": draw_partner(jax.random.fold_in(splits[5], 71), 0),
        "kernel_index": set_ends(jax.random.randint(splits[4], (NKPT, NKPT), 0, NKERN), jax.random.fold_in(splits[4], 1), 0, NKERN - 1).astype(jnp.int32),
    }


def spectral(real_part, imag_part, inverse):
    shaped = real_part.shape[:-2] + (GRID, GRID, GRID)
    complex_field = lax.complex(real_part, imag_part).reshape(shaped)
    if inverse:
        output = jnp.fft.ifftn(complex_field, axes=(-3, -2, -1), norm="ortho")
    else:
        output = jnp.fft.fftn(complex_field, axes=(-3, -2, -1), norm="ortho")
    return jnp.real(output).reshape(real_part.shape), jnp.imag(output).reshape(real_part.shape)


def reference(targets, occupied, kernels, partner, kernel_index):
    per_kpoint = N_BAND // KPT_DEV
    group_targets = KPT_DEV * NTGT_K

    def one_group(group_number):
        partner_group = partner[group_number]
        target_block = lax.dynamic_slice_in_dim(targets, group_number * group_targets, group_targets, 0)
        occupied_block = lax.dynamic_slice_in_dim(occupied, partner_group * N_BAND, N_BAND, 0).astype(jnp.float32)
        target_k = group_number * KPT_DEV + jnp.arange(group_targets, dtype=jnp.int32) // NTGT_K
        target_real = target_block[:, 0]
        target_imag = target_block[:, 1]

        def visit(totals, visited):
            orbital, source_band = visited
            source_k = partner_group * KPT_DEV + source_band // per_kpoint
            kernel = kernels[kernel_index[target_k, source_k]]
            orbital_real = orbital[0]
            orbital_imag = orbital[1]
            dens_real = orbital_real * target_real + orbital_imag * target_imag
            dens_imag = orbital_real * target_imag - orbital_imag * target_real
            spec_real, spec_imag = spectral(dens_real, dens_imag, False)
            pot_real, pot_imag = spectral(kernel * spec_real, kernel * spec_imag, True)
            new_real = totals[0] - (orbital_real * pot_real - orbital_imag * pot_imag)
            new_imag = totals[1] - (orbital_real * pot_imag + orbital_imag * pot_real)
            return (new_real, new_imag), None

        blank = jnp.zeros(target_real.shape, jnp.float32)
        totals, unused = lax.scan(visit, (blank, blank), (occupied_block, jnp.arange(N_BAND, dtype=jnp.int32)))
        return jnp.stack(totals, axis=1)

    result = lax.map(one_group, jnp.arange(N_KA, dtype=jnp.int32))
    return result.reshape(targets.shape)
```

```python
import functools
import math

import jax
import jax.numpy as jnp
import ml_dtypes
import numpy as np
from jax import lax
from jax.experimental import pallas as pl
from jax.experimental.pallas import tpu as pltpu
from jax.sharding import PartitionSpec as P

KPT_DEV = 2
RADIX = 3
CHUNK = 8
BF16 = jnp.bfloat16
F32 = jnp.float32


def split_table(table):
    high = table.astype(ml_dtypes.bfloat16)
    low = (table - high.astype(np.float64)).astype(ml_dtypes.bfloat16)
    return high, low


def plane_tables(grid_size):
    inner = grid_size // RADIX
    b, c = np.divmod(np.arange(inner * grid_size), grid_size)
    found = []
    for residue in range(RADIX):
        turns = b[:, None] * (RADIX * b[None, :] + residue) + c[:, None] * c[None, :]
        angles = (turns % grid_size) * (2.0 * np.pi / grid_size)
        found.append([split_table(np.cos(angles)), split_table(np.sin(angles))])
    forward = np.array(found)
    return np.stack([forward, np.swapaxes(forward, -1, -2)])


def line_tables(grid_size):
    positions = np.arange(grid_size)
    angles = (positions[:, None] * positions[None, :] % grid_size) * (2.0 * np.pi / grid_size)
    found = []
    for sign in (1.0, -1.0):
        full = np.block(
            [
                [np.cos(angles), sign * np.sin(angles)],
                [-sign * np.sin(angles), np.cos(angles)],
            ]
        )
        high, low = split_table(full)
        found.append(np.concatenate([high, high, low], axis=1))
    return np.stack(found)


def halves(values):
    high = values.astype(BF16)
    return high, (values - high.astype(F32)).astype(BF16)


def dot(left, right):
    return jnp.dot(left, right, preferred_element_type=F32)


def line_transform(values, table):
    high, low = halves(values)
    return dot(table, jnp.concatenate([high, low, high], axis=0))


def plane_transform(batch, tables, sign):
    rows = batch[0].shape[0]
    half = rows // 2
    high, low = halves(jnp.concatenate(batch, axis=0))
    parts = []
    for which in range(2):
        table_high, table_low = tables[which]
        parts.append(dot(high, table_high) + dot(low, table_high) + dot(high, table_low))
    found = []
    for number in range(len(batch)):
        at = number * rows
        cosine = parts[0][at : at + rows]
        sine = parts[1][at : at + rows]
        found.append(
            jnp.concatenate(
                [
                    cosine[:half] + sign * sine[half:],
                    cosine[half:] - sign * sine[:half],
                ],
                axis=0,
            )
        )
    return found


def butterfly(first, second, third, sign):
    half = first.shape[0] // 2
    total = second + third
    turned = (second - third) * (math.sqrt(3.0) / 2.0)
    middle = first - 0.5 * total
    turned = jnp.concatenate([sign * turned[half:], -sign * turned[:half]], axis=0)
    return first + total, middle + turned, middle - turned


def prepare_body(partner_ref, index_ref, kernels_ref, out_ref, held, sems):
    group = lax.axis_index("ka")
    per_kpoint = lax.axis_size("band") // KPT_DEV
    kpoint = group * KPT_DEV + lax.axis_index("band") // per_kpoint
    grid_size = kernels_ref.shape[1]
    inner = grid_size // RADIX
    copies = []
    for local in range(KPT_DEV):
        row = index_ref[kpoint, partner_ref[group] * KPT_DEV + local]
        copy = pltpu.make_async_copy(kernels_ref.at[row], held.at[local], sems.at[local])
        copy.start()
        copies.append(copy)
    for copy in copies:
        copy.wait()
    scale = 1.0 / grid_size**3
    for local in range(KPT_DEV):
        values = held[local] * scale
        for residue in range(RADIX):
            blocks = []
            for q in range(inner):
                at = (RADIX * q + residue) * grid_size
                blocks.append(values[:, at : at + grid_size])
            out_ref[local, residue] = jnp.concatenate(blocks, axis=1)


def prepare(partner, kernel_index, kernels):
    grid_size, plane = kernels.shape[1:]
    return pl.pallas_call(
        prepare_body,
        out_shape=jax.ShapeDtypeStruct((KPT_DEV, RADIX, grid_size, plane // RADIX), F32),
        in_specs=[
            pl.BlockSpec(memory_space=pltpu.SMEM),
            pl.BlockSpec(memory_space=pltpu.SMEM),
            pl.BlockSpec(memory_space=pl.ANY),
        ],
        out_specs=pl.BlockSpec(memory_space=pltpu.VMEM),
        scratch_shapes=[
            pltpu.VMEM((KPT_DEV, grid_size, plane), F32),
            pltpu.SemaphoreType.DMA((KPT_DEV,)),
        ],
    )(partner, kernel_index, kernels)


def exchange_body(sources, target_ref, orbital_ref, kernel_ref, line_ref, plane_ref, out_ref):
    grid_size, plane = target_ref.shape[2:]
    width = plane // RADIX
    per_kpoint = lax.axis_size("band") // KPT_DEV
    position = lax.axis_index("band")
    lanes = [slice(block * width, (block + 1) * width) for block in range(RADIX)]
    target = [(target_ref[0, 0][:, at], target_ref[0, 1][:, at]) for at in lanes]

    def orbital_of(number):
        return [
            (orbital_ref[number, 0][:, at].astype(F32), orbital_ref[number, 1][:, at].astype(F32))
            for at in lanes
        ]

    def some(numbers, totals):
        fields = [[] for _ in range(RADIX)]
        for number in numbers:
            blocks = []
            for (real, imag), (target_real, target_imag) in zip(orbital_of(number), target):
                blocks.append(
                    jnp.concatenate(
                        [
                            real * target_real + imag * target_imag,
                            real * target_imag - imag * target_real,
                        ],
                        axis=0,
                    )
                )
            for residue, block in enumerate(butterfly(*blocks, 1.0)):
                fields[residue].append(block)
        for residue in range(RADIX):
            tables = [[plane_ref[0, residue, i, j] for j in range(2)] for i in range(2)]
            batch = plane_transform(fields[residue], tables, 1.0)
            for place, number in enumerate(numbers):
                local = sources(position, number) // per_kpoint
                kernel = kernel_ref[local, residue]
                values = line_transform(batch[place], line_ref[0])
                values = values * jnp.concatenate([kernel, kernel], axis=0)
                batch[place] = line_transform(values, line_ref[1])
            tables = [[plane_ref[1, residue, i, j] for j in range(2)] for i in range(2)]
            fields[residue] = plane_transform(batch, tables, -1.0)
        for place, number in enumerate(numbers):
            blocks = butterfly(*[fields[residue][place] for residue in range(RADIX)], -1.0)
            for block, (real, imag) in enumerate(orbital_of(number)):
                pot_real, pot_imag = blocks[block][:grid_size], blocks[block][grid_size:]
                totals[block] = (
                    totals[block][0] - (real * pot_real - imag * pot_imag),
                    totals[block][1] - (real * pot_imag + imag * pot_real),
                )
        return totals

    blank = jnp.zeros((grid_size, width), F32)
    totals = [(blank, blank) for _ in range(RADIX)]
    count = orbital_ref.shape[0]
    for start in range(0, count, CHUNK):
        totals = some(range(start, min(start + CHUNK, count)), totals)
    for part in range(2):
        out_ref[0, part] = jnp.concatenate([totals[block][part] for block in range(RADIX)], axis=1)


def exchange(sources, target, orbitals, kernels):
    grid_size = target.shape[2]
    return pl.pallas_call(
        functools.partial(exchange_body, sources),
        out_shape=jax.ShapeDtypeStruct(target.shape, F32),
        in_specs=[pl.BlockSpec(memory_space=pltpu.VMEM)] * 5,
        out_specs=pl.BlockSpec(memory_space=pltpu.VMEM),
        compiler_params=pltpu.CompilerParams(vmem_limit_bytes=32 * 1024 * 1024),
    )(target, orbitals, kernels, jnp.asarray(line_tables(grid_size)), jnp.asarray(plane_tables(grid_size)))


def shards(targets, occupied, kernels, partner, kernel_index):
    groups = lax.axis_size("ka")
    band_count = lax.axis_size("band")
    my_group = lax.axis_index("ka")
    kernel_blocks = prepare(partner, kernel_index, kernels)

    shift = (partner[my_group] - my_group) % groups
    visitor = occupied
    for by in range(1, groups):
        came = lax.ppermute(occupied, "ka", [((i + by) % groups, i) for i in range(groups)])
        visitor = jnp.where(shift == by, came, visitor)

    chips = band_count // 2
    visitors = [visitor]
    for step in range(1, chips):
        visitors.append(lax.ppermute(visitor, "band", [(i, i ^ (2 * step)) for i in range(band_count)]))
    stacked = jnp.concatenate(visitors, axis=0)
    others = lax.ppermute(stacked, "band", [(i, i ^ 1) for i in range(band_count)])
    orbitals = jnp.concatenate([stacked, others], axis=0)

    def sources(position, number):
        return position ^ (2 * (number % chips)) ^ (number // chips)

    return exchange(sources, targets, orbitals, kernel_blocks)


def solution(mesh):
    return jax.shard_map(
        shards,
        mesh=mesh,
        in_specs=(
            P(("ka", "band"), None, None, None),
            P(("ka", "band"), None, None, None),
            P(),
            P(),
            P(),
        ),
        out_specs=P(("ka", "band"), None, None, None),
        check_vma=False,
    )
```

```python
import functools
import math

import jax
import jax.numpy as jnp
import ml_dtypes
import numpy as np
from jax import lax
from jax.experimental import pallas as pl
from jax.experimental.pallas import tpu as pltpu
from jax.sharding import PartitionSpec as P

KPT_DEV = 2
RADIX = 6
CHUNK = 8
LANES = 128
PITCH_GAP = 0
CARRIED = 3
SCOPED_BYTES = 16 * 1024 * 1024
BF16 = jnp.bfloat16
F32 = jnp.float32


def split_table(table):
    high = table.astype(ml_dtypes.bfloat16)
    low = (table - high.astype(np.float64)).astype(ml_dtypes.bfloat16)
    return high, low


def padded(width):
    return -(-width // LANES) * LANES


def plane_tables(grid_size):
    inner = grid_size // RADIX
    width = inner * grid_size
    room = padded(width) - width
    b, c = np.divmod(np.arange(width), grid_size)
    found = []
    for sign in (1.0, -1.0):
        for residue in range(RADIX):
            turns = b[:, None] * (RADIX * b[None, :] + residue) + c[:, None] * c[None, :]
            angles = (turns % grid_size) * (2.0 * np.pi / grid_size)
            if sign < 0:
                angles = angles.T
            cosine = np.pad(np.cos(angles), [(0, room)] * 2)
            sine = np.pad(sign * np.sin(angles), [(0, room)] * 2)
            found.append(split_table(np.block([[cosine, -sine], [sine, cosine]])))
    found = np.array(found)
    return found.reshape((2, RADIX) + found.shape[1:])


def halves(values):
    high = values.astype(BF16)
    return high, (values - high.astype(F32)).astype(BF16)


def plane_transform(real, imag, tables):
    high, low = halves(jnp.concatenate([jnp.concatenate(real, axis=0), jnp.concatenate(imag, axis=0)], axis=1))
    left = jnp.concatenate([high, low, high], axis=1)
    right = jnp.concatenate([tables[0], tables[0], tables[1]], axis=0)
    found = jnp.dot(left, right, preferred_element_type=F32)
    half = found.shape[1] // 2
    return found[:, :half], found[:, half:]


def turn(value, angle):
    real, imag = value
    eighths = angle * 8
    if eighths == int(eighths):
        eighth = int(eighths) % 8
        if eighth % 2:
            half = math.sqrt(0.5)
            real, imag = (real + imag) * half, (imag - real) * half
        for _ in range(eighth // 2):
            real, imag = imag, -real
        return real, imag
    cosine, sine = math.cos(2 * math.pi * angle), math.sin(2 * math.pi * angle)
    return real * cosine + imag * sine, imag * cosine - real * sine


def plus(left, right):
    return left[0] + right[0], left[1] + right[1]


def minus(left, right):
    return left[0] - right[0], left[1] - right[1]


def three_points(first, second, third, sign):
    total = plus(second, third)
    apart = minus(second, third)
    factor = sign * math.sqrt(3.0) / 2.0
    turned = (apart[1] * factor, apart[0] * -factor)
    middle = (first[0] - 0.5 * total[0], first[1] - 0.5 * total[1])
    return [plus(first, total), plus(middle, turned), minus(middle, turned)]


def line_transform(values, sign):
    size = len(values)
    if size == 1:
        return values
    if size == 3:
        return three_points(*values, sign)
    odd = size
    while odd % 2 == 0:
        odd //= 2
    if odd == 1:
        even = line_transform(values[0::2], sign)
        other = line_transform(values[1::2], sign)
        other = [turn(value, sign * k / size) for k, value in enumerate(other)]
        return [plus(*both) for both in zip(even, other)] + [minus(*both) for both in zip(even, other)]
    if odd == size:
        found = []
        for k in range(size):
            total = values[0]
            for n in range(1, size):
                total = plus(total, turn(values[n], sign * (k * n % size) / size))
            found.append(total)
        return found
    twos = size // odd
    rows = []
    for i in range(odd):
        rows.append(line_transform([values[(twos * i + odd * j) % size] for j in range(twos)], sign))
    columns = [line_transform([row[j] for row in rows], sign) for j in range(twos)]
    return [columns[k % twos][k % odd] for k in range(size)]


def prepare_body(steps, partner_ref, index_ref, kernels_ref, *refs):
    carried, (out_ref, shift_ref), refs = refs[:CARRIED], refs[CARRIED : CARRIED + 2], refs[CARRIED + 2 :]
    copied, (partner, index, held, sems) = refs[:CARRIED], refs[CARRIED:]
    copies = []
    moves = [(partner_ref, partner), (index_ref, index), (kernels_ref, held), *zip(carried, copied)]
    for number, (source, target) in enumerate(moves):
        copy = pltpu.make_async_copy(source, target, sems.at[number])
        copy.start()
        copies.append(copy)
    group = lax.axis_index("ka")
    position = lax.axis_index("band")
    per_kpoint = lax.axis_size("band") // KPT_DEV
    kpoint = group * KPT_DEV + position // per_kpoint
    grid_size = kernels_ref.shape[1]
    inner = grid_size // RADIX
    width = inner * grid_size
    slots = lax.broadcasted_iota(jnp.int32, (CHUNK, LANES), 0)
    chosen = []
    for start in range(0, len(steps), CHUNK):
        local_of = jnp.zeros((CHUNK, LANES), jnp.int32)
        for slot, step in enumerate(steps[start : start + CHUNK]):
            local = (position ^ (2 * step)) // per_kpoint
            local_of = jnp.where(slots == slot, local, local_of)
        chosen.append([local_of == local for local in range(KPT_DEV)])
    for copy in copies[:3]:
        copy.wait()
    groups = lax.axis_size("ka")
    shift_ref[0] = lax.rem(partner[group] + groups - group, groups)
    numbers = [index[kpoint, partner[group] * KPT_DEV + local] for local in range(KPT_DEV)]
    scale = 1.0 / grid_size**3
    for residue in range(RADIX):
        arranged = []
        for number in numbers:
            blocks = []
            for q in range(inner):
                at = (RADIX * q + residue) * grid_size
                blocks.append(held[number, :, at : at + grid_size])
            blocks.append(jnp.zeros((grid_size, padded(width) - width), F32))
            arranged.append(jnp.concatenate(blocks, axis=1) * scale)
        for lane in range(padded(width) // LANES):
            at = slice(lane * LANES, (lane + 1) * LANES)
            for p in range(grid_size):
                rows = [jnp.broadcast_to(values[p : p + 1, at], (CHUNK, LANES)) for values in arranged]
                for number, masks in enumerate(chosen):
                    found = rows[0]
                    for local in range(1, KPT_DEV):
                        found = jnp.where(masks[local], rows[local], found)
                    out_ref[number, residue, lane, p] = found
    for copy in copies[3:]:
        copy.wait()


def in_hbm(array):
    return pltpu.with_memory_space_constraint(array, pltpu.HBM)


def prepare(steps, partner, kernel_index, kernels, *carried):
    grid_size, plane = kernels.shape[1:]
    chunks = -(-len(steps) // CHUNK)
    lanes = padded(plane // RADIX) // LANES
    given = [partner, kernel_index, kernels, *carried]
    return pl.pallas_call(
        functools.partial(prepare_body, steps),
        out_shape=[
            pltpu.VMEM((chunks, RADIX, lanes, grid_size, CHUNK, LANES), F32),
            pltpu.SMEM((1,), jnp.int32),
            *[pltpu.VMEM(array.shape, array.dtype) for array in carried],
        ],
        in_specs=[pl.BlockSpec(memory_space=pltpu.HBM)] * len(given),
        out_specs=[
            pl.BlockSpec(memory_space=pltpu.VMEM),
            pl.BlockSpec(memory_space=pltpu.SMEM),
            *[pl.BlockSpec(memory_space=pltpu.VMEM)] * len(carried),
        ],
        scratch_shapes=[
            pltpu.SMEM(partner.shape, jnp.int32),
            pltpu.SMEM(kernel_index.shape, jnp.int32),
            pltpu.VMEM(kernels.shape, F32),
            pltpu.SemaphoreType.DMA((len(given),)),
        ],
        compiler_params=pltpu.CompilerParams(vmem_limit_bytes=SCOPED_BYTES),
    )(*[in_hbm(array) for array in given])


def choose_body(shift_ref, *refs):
    for by, ref in enumerate(refs[:-1]):

        @pl.when(shift_ref[0] == by)
        def _(ref=ref):
            refs[-1][...] = ref[...]


def choose(shift, arrays):
    whole = pl.BlockSpec(memory_space=pltpu.VMEM)
    return pl.pallas_call(
        choose_body,
        out_shape=pltpu.VMEM(arrays[0].shape, arrays[0].dtype),
        in_specs=[pl.BlockSpec(memory_space=pltpu.SMEM), *[whole] * len(arrays)],
        out_specs=whole,
        compiler_params=pltpu.CompilerParams(vmem_limit_bytes=SCOPED_BYTES),
    )(shift, *arrays)


def lane_blocks(values, width):
    rows, plane = values.shape
    found = []
    for block in range(RADIX):
        at, room = block * width, padded(width)
        if at + room <= plane:
            found.append(values[:, at : at + room])
        else:
            blank = jnp.zeros((rows, at + room - plane), values.dtype)
            found.append(jnp.concatenate([values[:, at:], blank], axis=1))
    return found


def forward(members, first, target_ref, plane_ref, field_ref, held_ref):
    grid_size, plane = target_ref.shape[2:]
    lanes = field_ref.shape[3]
    pitch = field_ref.shape[4] // CHUNK
    target = [lane_blocks(target_ref[0, part], plane // RADIX) for part in range(2)]
    taken = 0
    while taken < len(members):
        chunk, slot = divmod(first + taken, CHUNK)
        batch = members[taken : taken + CHUNK - slot]
        taken += len(batch)
        fields = [([], []) for _ in range(RADIX)]
        for place, (ref, row) in enumerate(batch):
            orbital = [
                [values.astype(F32) for values in lane_blocks(ref[row, part], plane // RADIX)] for part in range(2)
            ]
            blocks = []
            for block in range(RADIX):
                real, imag = orbital[0][block], orbital[1][block]
                target_real, target_imag = target[0][block], target[1][block]
                held_ref[chunk, slot + place, 0, block] = real
                held_ref[chunk, slot + place, 1, block] = imag
                blocks.append(
                    (
                        real * target_real + imag * target_imag,
                        real * target_imag - imag * target_real,
                    )
                )
            for residue, value in enumerate(line_transform(blocks, 1.0)):
                for part in range(2):
                    fields[residue][part].append(value[part])
        for residue in range(RADIX):
            parts = plane_transform(*fields[residue], [plane_ref[0, residue, j] for j in range(2)])
            for part in range(2):
                for place in range(len(batch)):
                    found = parts[part][place * grid_size : (place + 1) * grid_size]
                    for lane in range(lanes):
                        at = (slot + place) * pitch
                        field_ref[chunk, residue, part, lane, at : at + grid_size] = found[
                            :, lane * LANES : (lane + 1) * LANES
                        ]


def early_body(count, *refs):
    orbital_refs, (target_ref, plane_ref, field_ref, held_ref) = refs[:count], refs[count:]
    members = [(ref, row) for ref in orbital_refs for row in range(ref.shape[0])]
    forward(members, 0, target_ref, plane_ref, field_ref, held_ref)


def late_body(count, first, *refs):
    orbital_refs, refs = refs[:count], refs[count:]
    target_ref, plane_ref, kernel_ref, _, _, out_ref, field_ref, held_ref = refs
    grid_size, plane = target_ref.shape[2:]
    width = plane // RADIX
    chunks, _, _, lanes, rows = field_ref.shape[:5]
    pitch = rows // CHUNK
    members = [(ref, row) for ref in orbital_refs for row in range(ref.shape[0])]
    forward(members, first, target_ref, plane_ref, field_ref, held_ref)
    totals = [[0.0, 0.0] for _ in range(RADIX)]
    for chunk in range(chunks):
        potentials = []
        for residue in range(RADIX):
            for lane in range(lanes):
                values = [
                    tuple(field_ref[chunk, residue, part, lane, pl.ds(a, CHUNK, stride=pitch)] for part in range(2))
                    for a in range(grid_size)
                ]
                scaled = []
                for p, (real, imag) in enumerate(line_transform(values, 1.0)):
                    kernel = kernel_ref[chunk, residue, lane, p]
                    scaled.append((real * kernel, imag * kernel))
                for a, value in enumerate(line_transform(scaled, -1.0)):
                    for part in range(2):
                        field_ref[chunk, residue, part, lane, pl.ds(a, CHUNK, stride=pitch)] = value[part]
        for residue in range(RADIX):
            parts = []
            for part in range(2):
                parts.append([])
                for place in range(CHUNK):
                    at = slice(place * pitch, place * pitch + grid_size)
                    found = [field_ref[chunk, residue, part, lane, at] for lane in range(lanes)]
                    parts[part].append(jnp.concatenate(found, axis=1))
            potentials.append(plane_transform(*parts, [plane_ref[1, residue, j] for j in range(2)]))
        for place in range(CHUNK):
            at = slice(place * grid_size, (place + 1) * grid_size)
            blocks = line_transform([(real[at], imag[at]) for real, imag in potentials], -1.0)
            for block, (pot_real, pot_imag) in enumerate(blocks):
                real, imag = (held_ref[chunk, place, part, block] for part in range(2))
                totals[block][0] -= real * pot_real - imag * pot_imag
                totals[block][1] -= real * pot_imag + imag * pot_real
    for part in range(2):
        out_ref[0, part] = jnp.concatenate([totals[block][part][:, :width] for block in range(RADIX)], axis=1)


def exchange(early, late, target, kernels, tables):
    grid_size, plane = target.shape[2:]
    lanes = padded(plane // RADIX) // LANES
    chunks = kernels.shape[0]
    known = sum(array.shape[0] for array in early)
    carried = [
        pltpu.VMEM((chunks, RADIX, 2, lanes, CHUNK * (grid_size + PITCH_GAP), LANES), F32),
        pltpu.VMEM((chunks, CHUNK, 2, RADIX, grid_size, lanes * LANES), F32),
    ]
    whole = pl.BlockSpec(memory_space=pltpu.VMEM)
    params = pltpu.CompilerParams(vmem_limit_bytes=SCOPED_BYTES)
    given = [*early, target, tables]
    field, held = pl.pallas_call(
        functools.partial(early_body, len(early)),
        out_shape=carried,
        in_specs=[whole] * len(given),
        out_specs=[whole] * 2,
        compiler_params=params,
    )(*given)
    given = [*late, target, tables, kernels, field, held]
    return pl.pallas_call(
        functools.partial(late_body, len(late), known),
        out_shape=[jax.ShapeDtypeStruct(target.shape, F32), *carried],
        in_specs=[whole] * len(given),
        out_specs=[whole] * 3,
        input_output_aliases={len(given) - 2: 1, len(given) - 1: 2},
        compiler_params=params,
    )(*given)[0]


def shards(targets, occupied, kernels, partner, kernel_index):
    groups = lax.axis_size("ka")
    band_count = lax.axis_size("band")
    chips = band_count // 2

    steps = [0, *range(2, chips), 1] * 2
    tables = jnp.asarray(plane_tables(targets.shape[2]))
    kernel_blocks, shift, own, target, tables = prepare(
        steps, partner, kernel_index, kernels, occupied, targets, tables
    )
    came = [
        lax.ppermute(occupied, "ka", [((i + by) % groups, i) for i in range(groups)]) for by in range(1, groups)
    ]
    visitor = choose(shift, [own, *came])

    def along(array, by):
        return lax.ppermute(array, "band", [(i, i ^ by) for i in range(band_count)])

    mine = jnp.concatenate([visitor, *[along(visitor, 2 * step) for step in steps[1:chips]]], axis=0)
    others = along(mine, 1)
    return exchange([mine], [others], target, kernel_blocks, tables)


def solution(mesh):
    return jax.shard_map(
        shards,
        mesh=mesh,
        in_specs=(
            P(("ka", "band"), None, None, None),
            P(("ka", "band"), None, None, None),
            P(),
            P(),
            P(),
        ),
        out_specs=P(("ka", "band"), None, None, None),
        check_vma=False,
    )
```

```python
import functools
import math

import jax
import jax.numpy as jnp
import ml_dtypes
import numpy as np
from jax import lax
from jax.experimental import pallas as pl
from jax.experimental.pallas import tpu as pltpu
from jax.sharding import PartitionSpec as P

KPT_DEV = 2
RADIX = 6
BATCH = 4
LANES = 128
SUBLANES = 8
FOLD = SUBLANES // BATCH
CARRIED = 3
SCOPED_BYTES = 16 * 1024 * 1024
BF16 = jnp.bfloat16
F32 = jnp.float32


def split_table(table):
    high = table.astype(ml_dtypes.bfloat16)
    low = (table - high.astype(np.float64)).astype(ml_dtypes.bfloat16)
    return high, low


def padded(width):
    return -(-width // LANES) * LANES


def plane_tables(grid_size):
    inner = grid_size // RADIX
    width = inner * grid_size
    room = padded(width) - width
    b, c = np.divmod(np.arange(width), grid_size)
    found = []
    for sign in (1.0, -1.0):
        for residue in range(RADIX):
            turns = b[:, None] * (RADIX * b[None, :] + residue) + c[:, None] * c[None, :]
            angles = (turns % grid_size) * (2.0 * np.pi / grid_size)
            if sign < 0:
                angles = angles.T
            cosine = np.pad(np.cos(angles), [(0, room)] * 2)
            sine = np.pad(sign * np.sin(angles), [(0, room)] * 2)
            found.append(split_table(np.block([[cosine, -sine], [sine, cosine]])))
    found = np.array(found)
    return found.reshape((2, RADIX) + found.shape[1:])


def halves(values):
    high = values.astype(BF16)
    return high, (values - high.astype(F32)).astype(BF16)


def plane_transform(real, imag, tables):
    high, low = halves(jnp.concatenate([real, imag], axis=1))
    count = high.shape[0]
    both = jnp.dot(jnp.concatenate([high, low], axis=0), tables[0], preferred_element_type=F32)
    found = both[:count] + (both[count:] + jnp.dot(high, tables[1], preferred_element_type=F32))
    half = found.shape[1] // 2
    return found[:, :half], found[:, half:]


def turn(value, angle):
    real, imag = value
    eighths = angle * 8
    if eighths == int(eighths):
        eighth = int(eighths) % 8
        if eighth % 2:
            half = math.sqrt(0.5)
            real, imag = (real + imag) * half, (imag - real) * half
        for _ in range(eighth // 2):
            real, imag = imag, -real
        return real, imag
    cosine, sine = math.cos(2 * math.pi * angle), math.sin(2 * math.pi * angle)
    return real * cosine + imag * sine, imag * cosine - real * sine


def plus(left, right):
    return left[0] + right[0], left[1] + right[1]


def minus(left, right):
    return left[0] - right[0], left[1] - right[1]


def three_points(first, second, third, sign):
    total = plus(second, third)
    apart = minus(second, third)
    factor = sign * math.sqrt(3.0) / 2.0
    turned = (apart[1] * factor, apart[0] * -factor)
    middle = (first[0] - 0.5 * total[0], first[1] - 0.5 * total[1])
    return [plus(first, total), plus(middle, turned), minus(middle, turned)]


def line_transform(values, sign):
    size = len(values)
    if size == 1:
        return values
    if size == 3:
        return three_points(*values, sign)
    odd = size
    while odd % 2 == 0:
        odd //= 2
    if odd == 1:
        even = line_transform(values[0::2], sign)
        other = line_transform(values[1::2], sign)
        other = [turn(value, sign * k / size) for k, value in enumerate(other)]
        return [plus(*both) for both in zip(even, other)] + [minus(*both) for both in zip(even, other)]
    if odd == size:
        found = []
        for k in range(size):
            total = values[0]
            for n in range(1, size):
                total = plus(total, turn(values[n], sign * (k * n % size) / size))
            found.append(total)
        return found
    twos = size // odd
    rows = []
    for i in range(odd):
        rows.append(line_transform([values[(twos * i + odd * j) % size] for j in range(twos)], sign))
    columns = [line_transform([row[j] for row in rows], sign) for j in range(twos)]
    return [columns[k % twos][k % odd] for k in range(size)]


def prepare_body(steps, partner_ref, index_ref, kernels_ref, *refs):
    carried, (out_ref, shift_ref), refs = refs[:CARRIED], refs[CARRIED : CARRIED + 2], refs[CARRIED + 2 :]
    copied, (partner, index, held, sems) = refs[:CARRIED], refs[CARRIED:]
    copies = []
    moves = [(partner_ref, partner), (index_ref, index), (kernels_ref, held), *zip(carried, copied)]
    for number, (source, target) in enumerate(moves):
        copy = pltpu.make_async_copy(source, target, sems.at[number])
        copy.start()
        copies.append(copy)
    group = lax.axis_index("ka")
    position = lax.axis_index("band")
    per_kpoint = lax.axis_size("band") // KPT_DEV
    kpoint = group * KPT_DEV + position // per_kpoint
    grid_size = kernels_ref.shape[1]
    inner = grid_size // RADIX
    width = inner * grid_size
    slots = lax.broadcasted_iota(jnp.int32, (SUBLANES, LANES), 0)
    chosen = []
    for start in range(0, len(steps), BATCH):
        local_of = jnp.zeros((SUBLANES, LANES), jnp.int32)
        for slot, step in enumerate(steps[start : start + BATCH] * FOLD):
            local = (position ^ (2 * step)) // per_kpoint
            local_of = jnp.where(slots == slot, local, local_of)
        chosen.append([local_of == local for local in range(KPT_DEV)])
    for copy in copies[:3]:
        copy.wait()
    shift_ref[0] = partner[group] ^ group
    numbers = [index[kpoint, partner[group] * KPT_DEV + local] for local in range(KPT_DEV)]
    scale = 1.0 / grid_size**3
    room = jnp.zeros((grid_size, padded(width) - width), F32)
    for residue in range(RADIX):
        fold, upper = divmod(residue, FOLD)
        arranged = []
        for number in numbers:
            blocks = []
            for q in range(inner):
                at = (RADIX * q + residue) * grid_size
                blocks.append(held[number, :, at : at + grid_size])
            arranged.append(jnp.concatenate([*blocks, room], axis=1) * scale)
        rows = slice(upper * BATCH, (upper + 1) * BATCH)
        for lane in range(padded(width) // LANES):
            at = slice(lane * LANES, (lane + 1) * LANES)
            for p in range(grid_size):
                values = [jnp.broadcast_to(value[p : p + 1, at], (SUBLANES, LANES)) for value in arranged]
                for batch, masks in enumerate(chosen):
                    found = values[0]
                    for local in range(1, KPT_DEV):
                        found = jnp.where(masks[local], values[local], found)
                    out_ref[batch, fold, lane, p, rows] = found[rows]
    for copy in copies[3:]:
        copy.wait()


def in_hbm(array):
    return pltpu.with_memory_space_constraint(array, pltpu.HBM)


def prepare(steps, partner, kernel_index, kernels, *carried):
    grid_size, plane = kernels.shape[1:]
    batches = len(steps) // BATCH
    lanes = padded(plane // RADIX) // LANES
    given = [partner, kernel_index, kernels, *carried]
    return pl.pallas_call(
        functools.partial(prepare_body, steps),
        out_shape=[
            pltpu.VMEM((batches, RADIX // FOLD, lanes, grid_size, SUBLANES, LANES), F32),
            pltpu.SMEM((1,), jnp.int32),
            *[pltpu.VMEM(array.shape, array.dtype) for array in carried],
        ],
        in_specs=[pl.BlockSpec(memory_space=pltpu.HBM)] * len(given),
        out_specs=[
            pl.BlockSpec(memory_space=pltpu.VMEM),
            pl.BlockSpec(memory_space=pltpu.SMEM),
            *[pl.BlockSpec(memory_space=pltpu.VMEM)] * len(carried),
        ],
        scratch_shapes=[
            pltpu.SMEM(partner.shape, jnp.int32),
            pltpu.SMEM(kernel_index.shape, jnp.int32),
            pltpu.VMEM(kernels.shape, F32),
            pltpu.SemaphoreType.DMA((len(given),)),
        ],
        compiler_params=pltpu.CompilerParams(vmem_limit_bytes=SCOPED_BYTES),
    )(*[in_hbm(array) for array in given])


def choose_body(shift_ref, *refs):
    for by, ref in enumerate(refs[:-1]):

        @pl.when(shift_ref[0] == by)
        def _(ref=ref):
            refs[-1][...] = ref[...]


def choose(shift, arrays):
    whole = pl.BlockSpec(memory_space=pltpu.VMEM)
    return pl.pallas_call(
        choose_body,
        out_shape=pltpu.VMEM(arrays[0].shape, arrays[0].dtype),
        in_specs=[pl.BlockSpec(memory_space=pltpu.SMEM), *[whole] * len(arrays)],
        out_specs=whole,
        compiler_params=pltpu.CompilerParams(vmem_limit_bytes=SCOPED_BYTES),
    )(shift, *arrays)


def lane_blocks(values, width):
    rows, plane = values.shape
    found = []
    for block in range(RADIX):
        at, room = block * width, padded(width)
        if at + room <= plane:
            found.append(values[:, at : at + room])
        else:
            blank = jnp.zeros((rows, at + room - plane), values.dtype)
            found.append(jnp.concatenate([values[:, at:], blank], axis=1))
    return found


def forward(refs, first, target_ref, plane_ref, kernel_ref, field_ref, held_ref, work_ref):
    grid_size, plane = target_ref.shape[2:]
    members = [(ref, row) for ref in refs for row in range(ref.shape[0])]
    lanes = field_ref.shape[4] // LANES
    count = BATCH * grid_size
    for start in range(0, len(members), BATCH):
        batch = (first + start) // BATCH
        for place, (ref, row) in enumerate(members[start : start + BATCH]):
            for part in range(2):
                for block, values in enumerate(lane_blocks(ref[row, part], plane // RADIX)):
                    held_ref[batch, place, part, block] = values.astype(F32)
        for tile in range(0, grid_size, SUBLANES):
            rows = slice(tile, tile + SUBLANES)
            target = [lane_blocks(target_ref[0, part, rows], plane // RADIX) for part in range(2)]
            for place in range(BATCH):
                blocks = []
                for block in range(RADIX):
                    real, imag = (held_ref[batch, place, part, block, rows] for part in range(2))
                    target_real, target_imag = target[0][block], target[1][block]
                    blocks.append(
                        (
                            real * target_real + imag * target_imag,
                            real * target_imag - imag * target_real,
                        )
                    )
                at = place * grid_size + tile
                for residue, value in enumerate(line_transform(blocks, 1.0)):
                    for part in range(2):
                        work_ref[residue, part, at : at + SUBLANES] = value[part]
        for fold in range(RADIX // FOLD):
            for upper in range(FOLD):
                residue = fold * FOLD + upper
                parts = [work_ref[residue, part, :count] for part in range(2)]
                parts = plane_transform(*parts, [plane_ref[0, residue, j] for j in range(2)])
                for part in range(2):
                    field_ref[batch, fold, part, upper * count : (upper + 1) * count] = parts[part]
            for lane in range(lanes):
                at = slice(lane * LANES, (lane + 1) * LANES)
                values = [
                    tuple(field_ref[batch, fold, part, pl.ds(a, SUBLANES, stride=grid_size), at] for part in range(2))
                    for a in range(grid_size)
                ]
                scaled = []
                for p, (real, imag) in enumerate(line_transform(values, 1.0)):
                    kernel = kernel_ref[batch, fold, lane, p]
                    scaled.append((real * kernel, imag * kernel))
                for a, value in enumerate(line_transform(scaled, -1.0)):
                    for part in range(2):
                        field_ref[batch, fold, part, pl.ds(a, SUBLANES, stride=grid_size), at] = value[part]


def early_body(count, *refs):
    forward(refs[:count], 0, *refs[count:])


def late_body(count, first, *refs):
    orbital_refs, refs = refs[:count], refs[count:]
    target_ref, plane_ref, kernel_ref, _, _, out_ref, field_ref, held_ref, work_ref = refs
    forward(orbital_refs, first, target_ref, plane_ref, kernel_ref, field_ref, held_ref, work_ref)
    grid_size, plane = target_ref.shape[2:]
    width = plane // RADIX
    batches = field_ref.shape[0]
    count = BATCH * grid_size
    for start in range(0, batches, 2):
        pair = range(start, min(start + 2, batches))
        for residue in range(RADIX):
            fold, upper = divmod(residue, FOLD)
            rows = slice(upper * count, (upper + 1) * count)
            parts = [
                jnp.concatenate([field_ref[batch, fold, part, rows] for batch in pair], axis=0) for part in range(2)
            ]
            parts = plane_transform(*parts, [plane_ref[1, residue, j] for j in range(2)])
            for part in range(2):
                work_ref[residue, part, : len(pair) * count] = parts[part]
        for tile in range(0, grid_size, SUBLANES):
            rows = slice(tile, tile + SUBLANES)
            totals = [[0.0, 0.0] for _ in range(RADIX)]
            for batch in pair:
                for place in range(BATCH):
                    at = (batch - start) * count + place * grid_size + tile
                    at = slice(at, at + SUBLANES)
                    blocks = line_transform(
                        [tuple(work_ref[residue, part, at] for part in range(2)) for residue in range(RADIX)], -1.0
                    )
                    for block, (pot_real, pot_imag) in enumerate(blocks):
                        real, imag = (held_ref[batch, place, part, block, rows] for part in range(2))
                        totals[block][0] -= real * pot_real - imag * pot_imag
                        totals[block][1] -= real * pot_imag + imag * pot_real
            for part in range(2):
                found = jnp.concatenate([totals[block][part][:, :width] for block in range(RADIX)], axis=1)
                out_ref[0, part, rows] = found if start == 0 else out_ref[0, part, rows] + found


def exchange(early, late, target, kernels, tables):
    grid_size, plane = target.shape[2:]
    room = padded(plane // RADIX)
    batches = kernels.shape[0]
    known = sum(array.shape[0] for array in early)
    carried = [
        pltpu.VMEM((batches, RADIX // FOLD, 2, SUBLANES * grid_size, room), F32),
        pltpu.VMEM((batches, BATCH, 2, RADIX, grid_size, room), F32),
    ]
    work = pltpu.VMEM((RADIX, 2, 2 * BATCH * grid_size, room), F32)
    whole = pl.BlockSpec(memory_space=pltpu.VMEM)
    params = pltpu.CompilerParams(vmem_limit_bytes=SCOPED_BYTES)
    given = [*early, target, tables, kernels]
    field, held = pl.pallas_call(
        functools.partial(early_body, len(early)),
        out_shape=carried,
        in_specs=[whole] * len(given),
        out_specs=[whole] * 2,
        scratch_shapes=[work],
        compiler_params=params,
    )(*given)
    given = [*late, target, tables, kernels, field, held]
    return pl.pallas_call(
        functools.partial(late_body, len(late), known),
        out_shape=[jax.ShapeDtypeStruct(target.shape, F32), *carried],
        in_specs=[whole] * len(given),
        out_specs=[whole] * 3,
        scratch_shapes=[work],
        input_output_aliases={len(given) - 2: 1, len(given) - 1: 2},
        compiler_params=params,
    )(*given)[0]


def shards(targets, occupied, kernels, partner, kernel_index):
    groups = lax.axis_size("ka")
    band_count = lax.axis_size("band")
    chips = band_count // 2

    steps = list(range(chips)) * 2
    tables = jnp.asarray(plane_tables(targets.shape[2]))
    kernel_blocks, shift, own, target, tables = prepare(
        steps, partner, kernel_index, kernels, occupied, targets, tables
    )
    came = [
        lax.ppermute(occupied, "ka", [(i ^ by, i) for i in range(groups)]) for by in range(1, groups)
    ]
    visitor = choose(shift, [own, *came])

    def along(array, by):
        return lax.ppermute(array, "band", [(i, i ^ by) for i in range(band_count)])

    mine = jnp.concatenate([visitor, *[along(visitor, 2 * step) for step in steps[1:chips]]], axis=0)
    others = along(mine, 1)
    return exchange([mine], [others], target, kernel_blocks, tables)


def solution(mesh):
    return jax.shard_map(
        shards,
        mesh=mesh,
        in_specs=(
            P(("ka", "band"), None, None, None),
            P(("ka", "band"), None, None, None),
            P(),
            P(),
            P(),
        ),
        out_specs=P(("ka", "band"), None, None, None),
        check_vma=False,
    )
```

```python
import functools
import math

import jax
import jax.numpy as jnp
import ml_dtypes
import numpy as np
from jax import lax
from jax.experimental import pallas as pl
from jax.experimental.pallas import tpu as pltpu
from jax.sharding import PartitionSpec as P

KPT_DEV = 2
RADIX = 6
BATCH = 4
LANES = 128
SUBLANES = 8
FOLD = SUBLANES // BATCH
CARRIED = 3
SCOPED_BYTES = 16 * 1024 * 1024
BF16 = jnp.bfloat16
F32 = jnp.float32


def split_table(table):
    high = table.astype(ml_dtypes.bfloat16)
    low = (table - high.astype(np.float64)).astype(ml_dtypes.bfloat16)
    return high, low


def padded(width):
    return -(-width // LANES) * LANES


def plane_tables(grid_size):
    inner = grid_size // RADIX
    width = inner * grid_size
    room = padded(width) - width
    b, c = np.divmod(np.arange(width), grid_size)
    found = []
    for sign in (1.0, -1.0):
        for residue in range(RADIX):
            turns = b[:, None] * (RADIX * b[None, :] + residue) + c[:, None] * c[None, :]
            angles = (turns % grid_size) * (2.0 * np.pi / grid_size)
            if sign < 0:
                angles = angles.T
            cosine = np.pad(np.cos(angles), [(0, room)] * 2)
            sine = np.pad(sign * np.sin(angles), [(0, room)] * 2)
            found.append(split_table(np.block([[cosine, -sine], [sine, cosine]])))
    found = np.array(found)
    return found.reshape((2, RADIX) + found.shape[1:])


def halves(values):
    high = values.astype(BF16)
    return high, (values - high.astype(F32)).astype(BF16)


def plane_transform(real, imag, tables):
    high, low = halves(jnp.concatenate([real, imag], axis=1))
    count = high.shape[0]
    both = jnp.dot(jnp.concatenate([high, low], axis=0), tables[0], preferred_element_type=F32)
    found = both[:count] + (both[count:] + jnp.dot(high, tables[1], preferred_element_type=F32))
    half = found.shape[1] // 2
    return found[:, :half], found[:, half:]


def turn(value, angle):
    real, imag = value
    eighths = angle * 8
    if eighths == int(eighths):
        eighth = int(eighths) % 8
        if eighth % 2:
            half = math.sqrt(0.5)
            real, imag = (real + imag) * half, (imag - real) * half
        for _ in range(eighth // 2):
            real, imag = imag, -real
        return real, imag
    cosine, sine = math.cos(2 * math.pi * angle), math.sin(2 * math.pi * angle)
    return real * cosine + imag * sine, imag * cosine - real * sine


def plus(left, right):
    return left[0] + right[0], left[1] + right[1]


def minus(left, right):
    return left[0] - right[0], left[1] - right[1]


def three_points(first, second, third, sign):
    total = plus(second, third)
    apart = minus(second, third)
    factor = sign * math.sqrt(3.0) / 2.0
    turned = (apart[1] * factor, apart[0] * -factor)
    middle = (first[0] - 0.5 * total[0], first[1] - 0.5 * total[1])
    return [plus(first, total), plus(middle, turned), minus(middle, turned)]


def line_transform(values, sign):
    size = len(values)
    if size == 1:
        return values
    if size == 3:
        return three_points(*values, sign)
    odd = size
    while odd % 2 == 0:
        odd //= 2
    if odd == 1:
        even = line_transform(values[0::2], sign)
        other = line_transform(values[1::2], sign)
        other = [turn(value, sign * k / size) for k, value in enumerate(other)]
        return [plus(*both) for both in zip(even, other)] + [minus(*both) for both in zip(even, other)]
    if odd == size:
        found = []
        for k in range(size):
            total = values[0]
            for n in range(1, size):
                total = plus(total, turn(values[n], sign * (k * n % size) / size))
            found.append(total)
        return found
    twos = size // odd
    rows = []
    for i in range(odd):
        rows.append(line_transform([values[(twos * i + odd * j) % size] for j in range(twos)], sign))
    columns = [line_transform([row[j] for row in rows], sign) for j in range(twos)]
    return [columns[k % twos][k % odd] for k in range(size)]


def prepare_body(steps, partner_ref, index_ref, kernels_ref, *refs):
    carried, (out_ref, shift_ref), refs = refs[:CARRIED], refs[CARRIED : CARRIED + 2], refs[CARRIED + 2 :]
    copied, (partner, index, held, sems) = refs[:CARRIED], refs[CARRIED:]
    copies = []
    moves = [(partner_ref, partner), (index_ref, index), (kernels_ref, held), *zip(carried, copied)]
    for number, (source, target) in enumerate(moves):
        copy = pltpu.make_async_copy(source, target, sems.at[number])
        copy.start()
        copies.append(copy)
    group = lax.axis_index("ka")
    position = lax.axis_index("band")
    per_kpoint = lax.axis_size("band") // KPT_DEV
    kpoint = group * KPT_DEV + position // per_kpoint
    grid_size = kernels_ref.shape[1]
    inner = grid_size // RADIX
    width = inner * grid_size
    slots = lax.broadcasted_iota(jnp.int32, (SUBLANES, LANES), 0)
    chosen = []
    for start in range(0, len(steps), BATCH):
        local_of = jnp.zeros((SUBLANES, LANES), jnp.int32)
        for slot, step in enumerate(steps[start : start + BATCH] * FOLD):
            local = (position ^ (2 * step)) // per_kpoint
            local_of = jnp.where(slots == slot, local, local_of)
        chosen.append([local_of == local for local in range(KPT_DEV)])
    for copy in copies[:3]:
        copy.wait()
    shift_ref[0] = partner[group] ^ group
    numbers = [index[kpoint, partner[group] * KPT_DEV + local] for local in range(KPT_DEV)]
    scale = 1.0 / grid_size**3
    room = jnp.zeros((grid_size, padded(width) - width), F32)
    for residue in range(RADIX):
        fold, upper = divmod(residue, FOLD)
        arranged = []
        for number in numbers:
            blocks = []
            for q in range(inner):
                at = (RADIX * q + residue) * grid_size
                blocks.append(held[number, :, at : at + grid_size])
            arranged.append(jnp.concatenate([*blocks, room], axis=1) * scale)
        rows = slice(upper * BATCH, (upper + 1) * BATCH)
        for lane in range(padded(width) // LANES):
            at = slice(lane * LANES, (lane + 1) * LANES)
            for p in range(grid_size):
                values = [jnp.broadcast_to(value[p : p + 1, at], (SUBLANES, LANES)) for value in arranged]
                for batch, masks in enumerate(chosen):
                    found = values[0]
                    for local in range(1, KPT_DEV):
                        found = jnp.where(masks[local], values[local], found)
                    out_ref[batch, fold, lane, p, rows] = found[rows]
    for copy in copies[3:]:
        copy.wait()


def in_hbm(array):
    return pltpu.with_memory_space_constraint(array, pltpu.HBM)


def prepare(steps, partner, kernel_index, kernels, *carried):
    grid_size, plane = kernels.shape[1:]
    batches = len(steps) // BATCH
    lanes = padded(plane // RADIX) // LANES
    given = [partner, kernel_index, kernels, *carried]
    return pl.pallas_call(
        functools.partial(prepare_body, steps),
        out_shape=[
            pltpu.VMEM((batches, RADIX // FOLD, lanes, grid_size, SUBLANES, LANES), F32),
            pltpu.SMEM((1,), jnp.int32),
            *[pltpu.VMEM(array.shape, array.dtype) for array in carried],
        ],
        in_specs=[pl.BlockSpec(memory_space=pltpu.HBM)] * len(given),
        out_specs=[
            pl.BlockSpec(memory_space=pltpu.VMEM),
            pl.BlockSpec(memory_space=pltpu.SMEM),
            *[pl.BlockSpec(memory_space=pltpu.VMEM)] * len(carried),
        ],
        scratch_shapes=[
            pltpu.SMEM(partner.shape, jnp.int32),
            pltpu.SMEM(kernel_index.shape, jnp.int32),
            pltpu.VMEM(kernels.shape, F32),
            pltpu.SemaphoreType.DMA((len(given),)),
        ],
        compiler_params=pltpu.CompilerParams(vmem_limit_bytes=SCOPED_BYTES),
    )(*[in_hbm(array) for array in given])


def choose_body(shifts, shift_ref, *refs):
    for by, ref in zip(shifts, refs[:-1]):

        @pl.when(shift_ref[0] == by)
        def _(ref=ref):
            refs[-1][...] = ref[...]


def choose(shift, shifts, arrays):
    whole = pl.BlockSpec(memory_space=pltpu.VMEM)
    return pl.pallas_call(
        functools.partial(choose_body, shifts),
        out_shape=pltpu.VMEM(arrays[0].shape, arrays[0].dtype),
        in_specs=[pl.BlockSpec(memory_space=pltpu.SMEM), *[whole] * len(arrays)],
        out_specs=whole,
        compiler_params=pltpu.CompilerParams(vmem_limit_bytes=SCOPED_BYTES),
    )(shift, *arrays)


def lane_blocks(values, width):
    rows, plane = values.shape
    found = []
    for block in range(RADIX):
        at, room = block * width, padded(width)
        if at + room <= plane:
            found.append(values[:, at : at + room])
        else:
            blank = jnp.zeros((rows, at + room - plane), values.dtype)
            found.append(jnp.concatenate([values[:, at:], blank], axis=1))
    return found


def exchange_body(count, first, started, *refs):
    orbital_refs, refs = refs[:count], refs[count:]
    target_ref, plane_ref, kernel_ref, refs = refs[0], refs[1], refs[2], refs[3:]
    out_ref, field_ref, held_ref, work_ref = refs[-4:]
    grid_size, plane = target_ref.shape[2:]
    width = plane // RADIX
    lanes = padded(width) // LANES
    size = BATCH * grid_size
    members = [(ref, row) for ref in orbital_refs for row in range(ref.shape[0])]
    for start in range(0, len(members), BATCH):
        batch = (first + start) // BATCH
        for place, (ref, row) in enumerate(members[start : start + BATCH]):
            for part in range(2):
                for block, values in enumerate(lane_blocks(ref[row, part], width)):
                    held_ref[place, part, block] = values.astype(F32)
        starts = {}
        for tile in range(0, grid_size, SUBLANES):
            rows = slice(tile, tile + SUBLANES)
            target = [lane_blocks(target_ref[0, part, rows], width) for part in range(2)]
            for place in range(BATCH):
                blocks = []
                for block in range(RADIX):
                    real, imag = (held_ref[place, part, block, rows] for part in range(2))
                    target_real, target_imag = target[0][block], target[1][block]
                    blocks.append(
                        (
                            real * target_real + imag * target_imag,
                            real * target_imag - imag * target_real,
                        )
                    )
                at = place * grid_size + tile
                for residue, value in enumerate(line_transform(blocks, 1.0)):
                    for part in range(2):
                        starts[residue, part, at] = value[part]
        def over_plane(fold):
            for upper in range(FOLD):
                residue = fold * FOLD + upper
                parts = [jnp.concatenate([starts[residue, part, at] for at in range(0, size, SUBLANES)], axis=0) for part in range(2)]
                parts = plane_transform(*parts, [plane_ref[0, residue, j] for j in range(2)])
                for part in range(2):
                    field_ref[fold, part, upper * size : (upper + 1) * size] = parts[part]

        def over_line(fold):
            for lane in range(lanes):
                at = slice(lane * LANES, (lane + 1) * LANES)
                values = [
                    tuple(field_ref[fold, part, pl.ds(a, SUBLANES, stride=grid_size), at] for part in range(2))
                    for a in range(grid_size)
                ]
                scaled = []
                for p, (real, imag) in enumerate(line_transform(values, 1.0)):
                    kernel = kernel_ref[batch, fold, lane, p]
                    scaled.append((real * kernel, imag * kernel))
                for a, value in enumerate(line_transform(scaled, -1.0)):
                    for part in range(2):
                        field_ref[fold, part, pl.ds(a, SUBLANES, stride=grid_size), at] = value[part]

        ends = {}

        def back(fold):
            for upper in range(FOLD):
                residue = fold * FOLD + upper
                parts = [field_ref[fold, part, upper * size : (upper + 1) * size] for part in range(2)]
                parts = plane_transform(*parts, [plane_ref[1, residue, j] for j in range(2)])
                ends[residue] = parts

        folds = RADIX // FOLD
        for turn_number in range(folds + 2):
            if turn_number < folds:
                over_plane(turn_number)
            if 0 <= turn_number - 1 < folds:
                over_line(turn_number - 1)
            if 0 <= turn_number - 2 < folds:
                back(turn_number - 2)
        for tile in range(0, grid_size, SUBLANES):
            rows = slice(tile, tile + SUBLANES)
            totals = [[0.0, 0.0] for _ in range(RADIX)]
            for place in range(BATCH):
                at = slice(place * grid_size + tile, place * grid_size + tile + SUBLANES)
                blocks = line_transform(
                    [tuple(ends[residue][part][at] for part in range(2)) for residue in range(RADIX)], -1.0
                )
                for block, (pot_real, pot_imag) in enumerate(blocks):
                    real, imag = (held_ref[place, part, block, rows] for part in range(2))
                    totals[block][0] -= real * pot_real - imag * pot_imag
                    totals[block][1] -= real * pot_imag + imag * pot_real
            for part in range(2):
                found = jnp.concatenate([totals[block][part][:, :width] for block in range(RADIX)], axis=1)
                if start:
                    found = out_ref[0, part, rows] + found
                elif started:
                    found = refs[0][0, part, rows] + found
                out_ref[0, part, rows] = found


def exchange(orbitals, first, target, tables, kernels, total=None):
    grid_size, plane = target.shape[2:]
    room = padded(plane // RADIX)
    given = [*orbitals, target, tables, kernels] + ([] if total is None else [total])
    whole = pl.BlockSpec(memory_space=pltpu.VMEM)
    return pl.pallas_call(
        functools.partial(exchange_body, len(orbitals), first, total is not None),
        out_shape=jax.ShapeDtypeStruct(target.shape, F32) if total is not None else pltpu.VMEM(target.shape, F32),
        in_specs=[whole] * len(given),
        out_specs=whole,
        scratch_shapes=[
            pltpu.VMEM((RADIX // FOLD, 2, SUBLANES * grid_size, room), F32),
            pltpu.VMEM((BATCH, 2, RADIX, grid_size, room), F32),
            pltpu.VMEM((RADIX, 2, BATCH * grid_size, room), F32),
        ],
        compiler_params=pltpu.CompilerParams(vmem_limit_bytes=SCOPED_BYTES),
    )(*given)


def shards(targets, occupied, kernels, partner, kernel_index):
    groups = lax.axis_size("ka")
    band_count = lax.axis_size("band")
    chips = band_count // 2

    steps = list(range(chips)) * 2
    tables = jnp.asarray(plane_tables(targets.shape[2]))
    kernel_blocks, shift, own, target, tables = prepare(
        steps, partner, kernel_index, kernels, occupied, targets, tables
    )
    shifts = list(range(groups - 1, 0, -1))
    came = [lax.ppermute(occupied, "ka", [(i ^ by, i) for i in range(groups)]) for by in shifts]
    visitor = choose(shift, [0, *shifts], [own, *came])

    def along(array, by):
        return lax.ppermute(array, "band", [(i, i ^ by) for i in range(band_count)])

    mine = jnp.concatenate([visitor, *[along(visitor, 2 * step) for step in steps[1:chips]]], axis=0)
    others = along(mine, 1)
    total = exchange([mine], 0, target, tables, kernel_blocks)
    return exchange([others], chips, target, tables, kernel_blocks, total)


def solution(mesh):
    return jax.shard_map(
        shards,
        mesh=mesh,
        in_specs=(
            P(("ka", "band"), None, None, None),
            P(("ka", "band"), None, None, None),
            P(),
            P(),
            P(),
        ),
        out_specs=P(("ka", "band"), None, None, None),
        check_vma=False,
    )
```

```python
import functools
import math

import jax
import jax.numpy as jnp
import ml_dtypes
import numpy as np
from jax import lax
from jax.experimental import pallas as pl
from jax.experimental.pallas import tpu as pltpu
from jax.sharding import PartitionSpec as P

KPT_DEV = 2
RADIX = 6
BATCH = 4
LANES = 128
SUBLANES = 8
FOLD = SUBLANES // BATCH
CARRIED = 3
SCOPED_BYTES = 16 * 1024 * 1024
BF16 = jnp.bfloat16
F32 = jnp.float32


def split_table(table):
    high = table.astype(ml_dtypes.bfloat16)
    low = (table - high.astype(np.float64)).astype(ml_dtypes.bfloat16)
    return high, low


def padded(width):
    return -(-width // LANES) * LANES


def plane_tables(grid_size):
    inner = grid_size // RADIX
    width = inner * grid_size
    room = padded(width) - width
    b, c = np.divmod(np.arange(width), grid_size)
    found = []
    for sign in (1.0, -1.0):
        for residue in range(RADIX):
            turns = b[:, None] * (RADIX * b[None, :] + residue) + c[:, None] * c[None, :]
            angles = (turns % grid_size) * (2.0 * np.pi / grid_size)
            if sign < 0:
                angles = angles.T
            cosine = np.pad(np.cos(angles), [(0, room)] * 2)
            sine = np.pad(sign * np.sin(angles), [(0, room)] * 2)
            found.append(split_table(np.block([[cosine, -sine], [sine, cosine]])))
    found = np.array(found)
    return found.reshape((2, RADIX) + found.shape[1:])


def halves(values):
    high = values.astype(BF16)
    return high, (values - high.astype(F32)).astype(BF16)


def plane_transform(real, imag, tables):
    high, low = halves(jnp.concatenate([real, imag], axis=1))
    count = high.shape[0]
    both = jnp.dot(jnp.concatenate([high, low], axis=0), tables[0], preferred_element_type=F32)
    found = both[:count] + (both[count:] + jnp.dot(high, tables[1], preferred_element_type=F32))
    half = found.shape[1] // 2
    return found[:, :half], found[:, half:]


def turn(value, angle):
    real, imag = value
    eighths = angle * 8
    if eighths == int(eighths):
        eighth = int(eighths) % 8
        if eighth % 2:
            half = math.sqrt(0.5)
            real, imag = (real + imag) * half, (imag - real) * half
        for _ in range(eighth // 2):
            real, imag = imag, -real
        return real, imag
    cosine, sine = math.cos(2 * math.pi * angle), math.sin(2 * math.pi * angle)
    return real * cosine + imag * sine, imag * cosine - real * sine


def plus(left, right):
    return left[0] + right[0], left[1] + right[1]


def minus(left, right):
    return left[0] - right[0], left[1] - right[1]


def three_points(first, second, third, sign):
    total = plus(second, third)
    apart = minus(second, third)
    factor = sign * math.sqrt(3.0) / 2.0
    turned = (apart[1] * factor, apart[0] * -factor)
    middle = (first[0] - 0.5 * total[0], first[1] - 0.5 * total[1])
    return [plus(first, total), plus(middle, turned), minus(middle, turned)]


def line_transform(values, sign):
    size = len(values)
    if size == 1:
        return values
    if size == 3:
        return three_points(*values, sign)
    odd = size
    while odd % 2 == 0:
        odd //= 2
    if odd == 1:
        even = line_transform(values[0::2], sign)
        other = line_transform(values[1::2], sign)
        other = [turn(value, sign * k / size) for k, value in enumerate(other)]
        return [plus(*both) for both in zip(even, other)] + [minus(*both) for both in zip(even, other)]
    if odd == size:
        found = []
        for k in range(size):
            total = values[0]
            for n in range(1, size):
                total = plus(total, turn(values[n], sign * (k * n % size) / size))
            found.append(total)
        return found
    twos = size // odd
    rows = []
    for i in range(odd):
        rows.append(line_transform([values[(twos * i + odd * j) % size] for j in range(twos)], sign))
    columns = [line_transform([row[j] for row in rows], sign) for j in range(twos)]
    return [columns[k % twos][k % odd] for k in range(size)]


def prepare_body(steps, partner_ref, index_ref, kernels_ref, *refs):
    carried, (out_ref, shift_ref), refs = refs[:CARRIED], refs[CARRIED : CARRIED + 2], refs[CARRIED + 2 :]
    copied, (partner, index, held, sems) = refs[:CARRIED], refs[CARRIED:]
    copies = []
    moves = [(partner_ref, partner), (index_ref, index), (kernels_ref, held), *zip(carried, copied)]
    for number, (source, target) in enumerate(moves):
        copy = pltpu.make_async_copy(source, target, sems.at[number])
        copy.start()
        copies.append(copy)
    group = lax.axis_index("ka")
    position = lax.axis_index("band")
    per_kpoint = lax.axis_size("band") // KPT_DEV
    kpoint = group * KPT_DEV + position // per_kpoint
    grid_size = kernels_ref.shape[1]
    inner = grid_size // RADIX
    width = inner * grid_size
    slots = lax.broadcasted_iota(jnp.int32, (SUBLANES, LANES), 0)
    chosen = []
    for start in range(0, len(steps), BATCH):
        local_of = jnp.zeros((SUBLANES, LANES), jnp.int32)
        for slot, step in enumerate(steps[start : start + BATCH] * FOLD):
            local = (position ^ (2 * step)) // per_kpoint
            local_of = jnp.where(slots == slot, local, local_of)
        chosen.append([local_of == local for local in range(KPT_DEV)])
    for copy in copies[:3]:
        copy.wait()
    shift_ref[0] = partner[group] ^ group
    numbers = [index[kpoint, partner[group] * KPT_DEV + local] for local in range(KPT_DEV)]
    scale = 1.0 / grid_size**3
    room = jnp.zeros((grid_size, padded(width) - width), F32)
    for residue in range(RADIX):
        fold, upper = divmod(residue, FOLD)
        arranged = []
        for number in numbers:
            blocks = []
            for q in range(inner):
                at = (RADIX * q + residue) * grid_size
                blocks.append(held[number, :, at : at + grid_size])
            arranged.append(jnp.concatenate([*blocks, room], axis=1) * scale)
        rows = slice(upper * BATCH, (upper + 1) * BATCH)
        for lane in range(padded(width) // LANES):
            at = slice(lane * LANES, (lane + 1) * LANES)
            for p in range(grid_size):
                values = [jnp.broadcast_to(value[p : p + 1, at], (SUBLANES, LANES)) for value in arranged]
                for batch, masks in enumerate(chosen):
                    found = values[0]
                    for local in range(1, KPT_DEV):
                        found = jnp.where(masks[local], values[local], found)
                    out_ref[batch, fold, lane, p, rows] = found[rows]
    for copy in copies[3:]:
        copy.wait()


def in_hbm(array):
    return pltpu.with_memory_space_constraint(array, pltpu.HBM)


def prepare(steps, partner, kernel_index, kernels, *carried):
    grid_size, plane = kernels.shape[1:]
    batches = len(steps) // BATCH
    lanes = padded(plane // RADIX) // LANES
    given = [partner, kernel_index, kernels, *carried]
    return pl.pallas_call(
        functools.partial(prepare_body, steps),
        out_shape=[
            pltpu.VMEM((batches, RADIX // FOLD, lanes, grid_size, SUBLANES, LANES), F32),
            pltpu.SMEM((1,), jnp.int32),
            *[pltpu.VMEM(array.shape, array.dtype) for array in carried],
        ],
        in_specs=[pl.BlockSpec(memory_space=pltpu.HBM)] * len(given),
        out_specs=[
            pl.BlockSpec(memory_space=pltpu.VMEM),
            pl.BlockSpec(memory_space=pltpu.SMEM),
            *[pl.BlockSpec(memory_space=pltpu.VMEM)] * len(carried),
        ],
        scratch_shapes=[
            pltpu.SMEM(partner.shape, jnp.int32),
            pltpu.SMEM(kernel_index.shape, jnp.int32),
            pltpu.VMEM(kernels.shape, F32),
            pltpu.SemaphoreType.DMA((len(given),)),
        ],
        compiler_params=pltpu.CompilerParams(vmem_limit_bytes=SCOPED_BYTES),
    )(*[in_hbm(array) for array in given])


def choose_body(shifts, shift_ref, *refs):
    for by, ref in zip(shifts, refs[:-1]):

        @pl.when(shift_ref[0] == by)
        def _(ref=ref):
            refs[-1][...] = ref[...]


def choose(shift, shifts, arrays):
    whole = pl.BlockSpec(memory_space=pltpu.VMEM)
    return pl.pallas_call(
        functools.partial(choose_body, shifts),
        out_shape=pltpu.VMEM(arrays[0].shape, arrays[0].dtype),
        in_specs=[pl.BlockSpec(memory_space=pltpu.SMEM), *[whole] * len(arrays)],
        out_specs=whole,
        compiler_params=pltpu.CompilerParams(vmem_limit_bytes=SCOPED_BYTES),
    )(shift, *arrays)


def lane_blocks(values, width):
    rows, plane = values.shape
    found = []
    for block in range(RADIX):
        at, room = block * width, padded(width)
        if at + room <= plane:
            found.append(values[:, at : at + room])
        else:
            blank = jnp.zeros((rows, at + room - plane), values.dtype)
            found.append(jnp.concatenate([values[:, at:], blank], axis=1))
    return found


def exchange_body(given, aims, first, started, *refs):
    orbital_refs, target_refs, refs = refs[:given], refs[given : given + aims], refs[given + aims :]
    plane_ref, kernel_ref, refs = refs[0], refs[1], refs[2:]
    total_refs, refs = refs[: aims * started], refs[aims * started :]
    out_refs, (field_ref, held_ref, work_ref) = refs[:aims], refs[aims:]
    grid_size, plane = target_refs[0].shape[2:]
    width = plane // RADIX
    lanes = padded(width) // LANES
    members = [(aim, ref, row) for aim in range(aims) for ref in orbital_refs for row in range(ref.shape[0])]
    written = set()
    for start in range(0, len(members), BATCH):
        batch = first + start // BATCH
        count = min(BATCH, len(members) - start)
        size = count * grid_size
        for place, (_, ref, row) in enumerate(members[start : start + count]):
            for part in range(2):
                for block, values in enumerate(lane_blocks(ref[row, part], width)):
                    held_ref[place, part, block] = values.astype(F32)
        starts = {}
        for tile in range(0, grid_size, SUBLANES):
            rows = slice(tile, tile + SUBLANES)
            targets = [[lane_blocks(ref[0, part, rows], width) for part in range(2)] for ref in target_refs]
            for place in range(count):
                blocks = []
                for block in range(RADIX):
                    real, imag = (held_ref[place, part, block, rows] for part in range(2))
                    target_real, target_imag = (targets[members[start + place][0]][part][block] for part in range(2))
                    blocks.append(
                        (
                            real * target_real + imag * target_imag,
                            real * target_imag - imag * target_real,
                        )
                    )
                at = place * grid_size + tile
                for residue, value in enumerate(line_transform(blocks, 1.0)):
                    for part in range(2):
                        starts[residue, part, at] = value[part]
        def over_plane(fold):
            for upper in range(FOLD):
                residue = fold * FOLD + upper
                parts = [jnp.concatenate([starts[residue, part, at] for at in range(0, size, SUBLANES)], axis=0) for part in range(2)]
                parts = plane_transform(*parts, [plane_ref[0, residue, j] for j in range(2)])
                for part in range(2):
                    field_ref[fold, part, upper * BATCH * grid_size : upper * BATCH * grid_size + size] = parts[part]

        def over_line(fold):
            for lane in range(lanes):
                at = slice(lane * LANES, (lane + 1) * LANES)
                values = [
                    tuple(field_ref[fold, part, pl.ds(a, SUBLANES, stride=grid_size), at] for part in range(2))
                    for a in range(grid_size)
                ]
                scaled = []
                for p, (real, imag) in enumerate(line_transform(values, 1.0)):
                    kernel = kernel_ref[batch, fold, lane, p]
                    scaled.append((real * kernel, imag * kernel))
                for a, value in enumerate(line_transform(scaled, -1.0)):
                    for part in range(2):
                        field_ref[fold, part, pl.ds(a, SUBLANES, stride=grid_size), at] = value[part]

        ends = {}

        def back(fold):
            for upper in range(FOLD):
                residue = fold * FOLD + upper
                parts = [field_ref[fold, part, upper * BATCH * grid_size : upper * BATCH * grid_size + size] for part in range(2)]
                parts = plane_transform(*parts, [plane_ref[1, residue, j] for j in range(2)])
                ends[residue] = parts

        folds = RADIX // FOLD
        for turn_number in range(folds + 2):
            if turn_number < folds:
                over_plane(turn_number)
            if 0 <= turn_number - 1 < folds:
                over_line(turn_number - 1)
            if 0 <= turn_number - 2 < folds:
                back(turn_number - 2)
        for tile in range(0, grid_size, SUBLANES):
            rows = slice(tile, tile + SUBLANES)
            totals = [[[0.0, 0.0] for _ in range(RADIX)] for _ in range(aims)]
            for place in range(count):
                aim = members[start + place][0]
                at = slice(place * grid_size + tile, place * grid_size + tile + SUBLANES)
                blocks = line_transform(
                    [tuple(ends[residue][part][at] for part in range(2)) for residue in range(RADIX)], -1.0
                )
                for block, (pot_real, pot_imag) in enumerate(blocks):
                    real, imag = (held_ref[place, part, block, rows] for part in range(2))
                    totals[aim][block][0] -= real * pot_real - imag * pot_imag
                    totals[aim][block][1] -= real * pot_imag + imag * pot_real
            for aim in sorted({members[start + place][0] for place in range(count)}):
                for part in range(2):
                    found = [totals[aim][block][part][:, :width] for block in range(RADIX)]
                    found = jnp.concatenate(found, axis=1)
                    if (aim, tile) in written:
                        found = out_refs[aim][0, part, rows] + found
                    elif started:
                        found = total_refs[aim][0, part, rows] + found
                    out_refs[aim][0, part, rows] = found
                written.add((aim, tile))


def exchange(orbitals, targets, first, tables, kernels, totals=(), **options):
    grid_size, plane = targets[0].shape[2:]
    room = padded(plane // RADIX)
    given = [*orbitals, *targets, tables, kernels, *totals]
    whole = pl.BlockSpec(memory_space=pltpu.VMEM)
    return pl.pallas_call(
        functools.partial(exchange_body, len(orbitals), len(targets), first, len(totals) > 0),
        out_shape=[pltpu.VMEM(array.shape, F32) for array in targets],
        in_specs=[whole] * len(given),
        out_specs=[whole] * len(targets),
        scratch_shapes=[
            pltpu.VMEM((RADIX // FOLD, 2, SUBLANES * grid_size, room), F32),
            pltpu.VMEM((BATCH, 2, RADIX, grid_size, room), F32),
            pltpu.VMEM((RADIX, 2, BATCH * grid_size, room), F32),
        ],
        compiler_params=pltpu.CompilerParams(vmem_limit_bytes=SCOPED_BYTES),
        **options,
    )(*given)


def shards(targets, occupied, kernels, partner, kernel_index):
    groups = lax.axis_size("ka")
    band_count = lax.axis_size("band")
    chips = band_count // 2

    def along(array, by):
        return lax.ppermute(array, "band", [(i, i ^ by) for i in range(band_count)])

    near_steps = list(range(chips - 2, 0, -1))
    steps = [0, chips - 1] * (BATCH // 2) + near_steps
    steps += [0] * (-len(steps) % BATCH)
    tables = jnp.asarray(plane_tables(targets.shape[2]))
    kernel_blocks, shift, own, target, tables = prepare(
        steps, partner, kernel_index, kernels, occupied, targets, tables
    )
    shifts = list(range(groups - 1, 0, -1))
    came = [lax.ppermute(occupied, "ka", [(i ^ by, i) for i in range(groups)]) for by in shifts]
    visitor = choose(shift, [0, *shifts], [own, *came])

    sibling = along(target, 1)
    early = [visitor, along(visitor, 2 * (chips - 1))]
    late = [along(visitor, 2 * step) for step in near_steps]
    free = pl.CostEstimate(flops=0, bytes_accessed=0, transcendentals=0)
    mine, other = exchange(early, [target, sibling], 0, tables, kernel_blocks, cost_estimate=free)
    (other,) = exchange(late, [sibling], 1, tables, kernel_blocks, [other])
    came = along(other, 1)
    (mine,) = exchange(late, [target], 1, tables, kernel_blocks, [mine])
    return mine + came


def solution(mesh):
    return jax.shard_map(
        shards,
        mesh=mesh,
        in_specs=(
            P(("ka", "band"), None, None, None),
            P(("ka", "band"), None, None, None),
            P(),
            P(),
            P(),
        ),
        out_specs=P(("ka", "band"), None, None, None),
        check_vma=False,
    )
```

```python
import functools
import math

import jax
import jax.numpy as jnp
import ml_dtypes
import numpy as np
from jax import lax
from jax.experimental import pallas as pl
from jax.experimental.pallas import tpu as pltpu
from jax.sharding import PartitionSpec as P

KPT_DEV = 2
RADIX = 6
BATCH = 4
LANES = 128
SUBLANES = 8
FOLD = SUBLANES // BATCH
CARRIED = 4
SCOPED_BYTES = 16 * 1024 * 1024
BF16 = jnp.bfloat16
F32 = jnp.float32


def split_table(table):
    high = table.astype(ml_dtypes.bfloat16)
    low = (table - high.astype(np.float64)).astype(ml_dtypes.bfloat16)
    return high, low


def padded(width):
    return -(-width // LANES) * LANES


def plane_tables(grid_size):
    inner = grid_size // RADIX
    width = inner * grid_size
    room = padded(width) - width
    b, c = np.divmod(np.arange(width), grid_size)
    turns = RADIX * b[:, None] * b[None, :] + c[:, None] * c[None, :]
    angles = (turns % grid_size) * (2.0 * np.pi / grid_size)
    cosine = np.pad(np.cos(angles), [(0, room)] * 2)
    sine = np.pad(np.sin(angles), [(0, room)] * 2)
    found = [split_table(np.block([[cosine, -sign * sine], [sign * sine, cosine]])) for sign in (1.0, -1.0)]
    return np.array(found)


def twist_tables(grid_size):
    width = grid_size // RADIX * grid_size
    b = np.pad(np.arange(width) // grid_size, (0, padded(width) - width))
    angles = np.arange(RADIX)[:, None] * b[None, :] * (2.0 * np.pi / grid_size)
    found = np.stack([np.cos(angles), np.sin(angles)], axis=1)
    return np.repeat(found[:, :, None], SUBLANES, axis=2).astype(np.float32)


def halves(values):
    high = values.astype(BF16)
    return high, (values - high.astype(F32)).astype(BF16)


def plane_transform(real, imag, tables):
    high, low = halves(jnp.concatenate([real, imag], axis=1))
    count = high.shape[0]
    both = jnp.dot(jnp.concatenate([high, low], axis=0), tables[0], preferred_element_type=F32)
    found = both[:count] + (both[count:] + jnp.dot(high, tables[1], preferred_element_type=F32))
    half = found.shape[1] // 2
    return found[:, :half], found[:, half:]


def turn(value, angle):
    real, imag = value
    eighths = angle * 8
    if eighths == int(eighths):
        eighth = int(eighths) % 8
        if eighth % 2:
            half = math.sqrt(0.5)
            real, imag = (real + imag) * half, (imag - real) * half
        for _ in range(eighth // 2):
            real, imag = imag, -real
        return real, imag
    cosine, sine = math.cos(2 * math.pi * angle), math.sin(2 * math.pi * angle)
    return real * cosine + imag * sine, imag * cosine - real * sine


def plus(left, right):
    return left[0] + right[0], left[1] + right[1]


def minus(left, right):
    return left[0] - right[0], left[1] - right[1]


def three_points(first, second, third, sign):
    total = plus(second, third)
    apart = minus(second, third)
    factor = sign * math.sqrt(3.0) / 2.0
    turned = (apart[1] * factor, apart[0] * -factor)
    middle = (first[0] - 0.5 * total[0], first[1] - 0.5 * total[1])
    return [plus(first, total), plus(middle, turned), minus(middle, turned)]


def line_transform(values, sign):
    size = len(values)
    if size == 1:
        return values
    if size == 3:
        return three_points(*values, sign)
    odd = size
    while odd % 2 == 0:
        odd //= 2
    if odd == 1:
        even = line_transform(values[0::2], sign)
        other = line_transform(values[1::2], sign)
        other = [turn(value, sign * k / size) for k, value in enumerate(other)]
        return [plus(*both) for both in zip(even, other)] + [minus(*both) for both in zip(even, other)]
    if odd == size:
        found = []
        for k in range(size):
            total = values[0]
            for n in range(1, size):
                total = plus(total, turn(values[n], sign * (k * n % size) / size))
            found.append(total)
        return found
    twos = size // odd
    rows = []
    for i in range(odd):
        rows.append(line_transform([values[(twos * i + odd * j) % size] for j in range(twos)], sign))
    columns = [line_transform([row[j] for row in rows], sign) for j in range(twos)]
    return [columns[k % twos][k % odd] for k in range(size)]


def prepare_body(steps, partner_ref, index_ref, kernels_ref, *refs):
    carried, (out_ref, shift_ref), refs = refs[:CARRIED], refs[CARRIED : CARRIED + 2], refs[CARRIED + 2 :]
    copied, (partner, index, held, sems) = refs[:CARRIED], refs[CARRIED:]
    copies = []
    moves = [(partner_ref, partner), (index_ref, index), (kernels_ref, held), *zip(carried, copied)]
    for number, (source, target) in enumerate(moves):
        copy = pltpu.make_async_copy(source, target, sems.at[number])
        copy.start()
        copies.append(copy)
    group = lax.axis_index("ka")
    position = lax.axis_index("band")
    per_kpoint = lax.axis_size("band") // KPT_DEV
    kpoint = group * KPT_DEV + position // per_kpoint
    grid_size = kernels_ref.shape[1]
    inner = grid_size // RADIX
    width = inner * grid_size
    slots = lax.broadcasted_iota(jnp.int32, (SUBLANES, LANES), 0)
    chosen = []
    for start in range(0, len(steps), BATCH):
        local_of = jnp.zeros((SUBLANES, LANES), jnp.int32)
        for slot, step in enumerate(steps[start : start + BATCH] * FOLD):
            local = (position ^ (2 * step)) // per_kpoint
            local_of = jnp.where(slots == slot, local, local_of)
        chosen.append([local_of == local for local in range(KPT_DEV)])
    for copy in copies[:3]:
        copy.wait()
    shift_ref[0] = partner[group] ^ group
    numbers = [index[kpoint, partner[group] * KPT_DEV + local] for local in range(KPT_DEV)]
    scale = 1.0 / grid_size**3
    room = jnp.zeros((grid_size, padded(width) - width), F32)
    for residue in range(RADIX):
        fold, upper = divmod(residue, FOLD)
        arranged = []
        for number in numbers:
            blocks = []
            for q in range(inner):
                at = (RADIX * q + residue) * grid_size
                blocks.append(held[number, :, at : at + grid_size])
            arranged.append(jnp.concatenate([*blocks, room], axis=1) * scale)
        rows = slice(upper * BATCH, (upper + 1) * BATCH)
        for lane in range(padded(width) // LANES):
            at = slice(lane * LANES, (lane + 1) * LANES)
            for p in range(grid_size):
                values = [jnp.broadcast_to(value[p : p + 1, at], (SUBLANES, LANES)) for value in arranged]
                for batch, masks in enumerate(chosen):
                    found = values[0]
                    for local in range(1, KPT_DEV):
                        found = jnp.where(masks[local], values[local], found)
                    out_ref[batch, fold, lane, p, rows] = found[rows]
    for copy in copies[3:]:
        copy.wait()


def in_hbm(array):
    return pltpu.with_memory_space_constraint(array, pltpu.HBM)


def prepare(steps, partner, kernel_index, kernels, *carried):
    grid_size, plane = kernels.shape[1:]
    batches = len(steps) // BATCH
    lanes = padded(plane // RADIX) // LANES
    given = [partner, kernel_index, kernels, *carried]
    return pl.pallas_call(
        functools.partial(prepare_body, steps),
        out_shape=[
            pltpu.VMEM((batches, RADIX // FOLD, lanes, grid_size, SUBLANES, LANES), F32),
            pltpu.SMEM((1,), jnp.int32),
            *[pltpu.VMEM(array.shape, array.dtype) for array in carried],
        ],
        in_specs=[pl.BlockSpec(memory_space=pltpu.HBM)] * len(given),
        out_specs=[
            pl.BlockSpec(memory_space=pltpu.VMEM),
            pl.BlockSpec(memory_space=pltpu.SMEM),
            *[pl.BlockSpec(memory_space=pltpu.VMEM)] * len(carried),
        ],
        scratch_shapes=[
            pltpu.SMEM(partner.shape, jnp.int32),
            pltpu.SMEM(kernel_index.shape, jnp.int32),
            pltpu.VMEM(kernels.shape, F32),
            pltpu.SemaphoreType.DMA((len(given),)),
        ],
        compiler_params=pltpu.CompilerParams(vmem_limit_bytes=SCOPED_BYTES),
    )(*[in_hbm(array) for array in given])


def choose_body(shifts, shift_ref, *refs):
    for by, ref in zip(shifts, refs[:-1]):

        @pl.when(shift_ref[0] == by)
        def _(ref=ref):
            refs[-1][...] = ref[...]


def choose(shift, shifts, arrays):
    whole = pl.BlockSpec(memory_space=pltpu.VMEM)
    return pl.pallas_call(
        functools.partial(choose_body, shifts),
        out_shape=pltpu.VMEM(arrays[0].shape, arrays[0].dtype),
        in_specs=[pl.BlockSpec(memory_space=pltpu.SMEM), *[whole] * len(arrays)],
        out_specs=whole,
        compiler_params=pltpu.CompilerParams(vmem_limit_bytes=SCOPED_BYTES),
    )(shift, *arrays)


def lane_blocks(values, width):
    rows, plane = values.shape
    found = []
    for block in range(RADIX):
        at, room = block * width, padded(width)
        if at + room <= plane:
            found.append(values[:, at : at + room])
        else:
            blank = jnp.zeros((rows, at + room - plane), values.dtype)
            found.append(jnp.concatenate([values[:, at:], blank], axis=1))
    return found


def exchange_body(given, aims, first, started, *refs):
    orbital_refs, target_refs, refs = refs[:given], refs[given : given + aims], refs[given + aims :]
    plane_ref, twist_ref, kernel_ref, refs = refs[0], refs[1], refs[2], refs[3:]
    total_refs, refs = refs[: aims * started], refs[aims * started :]
    out_refs, (field_ref, held_ref) = refs[:aims], refs[aims:]
    grid_size, plane = target_refs[0].shape[2:]
    width = plane // RADIX
    lanes = padded(width) // LANES
    members = [(aim, ref, row) for aim in range(aims) for ref in orbital_refs for row in range(ref.shape[0])]
    written = set()
    for start in range(0, len(members), BATCH):
        batch = first + start // BATCH
        count = min(BATCH, len(members) - start)
        size = count * grid_size
        for place, (_, ref, row) in enumerate(members[start : start + count]):
            for part in range(2):
                for block, values in enumerate(lane_blocks(ref[row, part], width)):
                    held_ref[place, part, block] = values.astype(F32)
        starts = {}
        for tile in range(0, grid_size, SUBLANES):
            rows = slice(tile, tile + SUBLANES)
            targets = [[lane_blocks(ref[0, part, rows], width) for part in range(2)] for ref in target_refs]
            for place in range(count):
                blocks = []
                for block in range(RADIX):
                    real, imag = (held_ref[place, part, block, rows] for part in range(2))
                    target_real, target_imag = (targets[members[start + place][0]][part][block] for part in range(2))
                    blocks.append(
                        (
                            real * target_real + imag * target_imag,
                            real * target_imag - imag * target_real,
                        )
                    )
                at = place * grid_size + tile
                for residue, (real, imag) in enumerate(line_transform(blocks, 1.0)):
                    if residue:
                        cosine, sine = twist_ref[residue, 0], twist_ref[residue, 1]
                        real, imag = real * cosine + imag * sine, imag * cosine - real * sine
                    starts[residue, 0, at], starts[residue, 1, at] = real, imag

        def over_plane(fold):
            residues = range(fold * FOLD, (fold + 1) * FOLD)
            places = [(residue, at) for residue in residues for at in range(0, size, SUBLANES)]
            parts = [jnp.concatenate([starts[residue, part, at] for residue, at in places], axis=0) for part in range(2)]
            parts = plane_transform(*parts, [plane_ref[0, j] for j in range(2)])
            for part in range(2):
                for upper in range(FOLD):
                    at = upper * BATCH * grid_size
                    field_ref[fold, part, at : at + size] = parts[part][upper * size : (upper + 1) * size]

        def over_line(fold):
            for lane in range(lanes):
                at = slice(lane * LANES, (lane + 1) * LANES)
                values = [
                    tuple(field_ref[fold, part, pl.ds(a, SUBLANES, stride=grid_size), at] for part in range(2))
                    for a in range(grid_size)
                ]
                scaled = []
                for p, (real, imag) in enumerate(line_transform(values, 1.0)):
                    kernel = kernel_ref[batch, fold, lane, p]
                    scaled.append((real * kernel, imag * kernel))
                for a, value in enumerate(line_transform(scaled, -1.0)):
                    for part in range(2):
                        field_ref[fold, part, pl.ds(a, SUBLANES, stride=grid_size), at] = value[part]

        ends = {}

        def back(fold):
            parts = []
            for part in range(2):
                at = [upper * BATCH * grid_size for upper in range(FOLD)]
                parts.append(jnp.concatenate([field_ref[fold, part, start : start + size] for start in at], axis=0))
            parts = plane_transform(*parts, [plane_ref[1, j] for j in range(2)])
            for upper in range(FOLD):
                ends[fold * FOLD + upper] = [values[upper * size : (upper + 1) * size] for values in parts]

        folds = RADIX // FOLD
        for turn_number in range(folds + 2):
            if turn_number < folds:
                over_plane(turn_number)
            if 0 <= turn_number - 1 < folds:
                over_line(turn_number - 1)
            if 0 <= turn_number - 2 < folds:
                back(turn_number - 2)
        for tile in range(0, grid_size, SUBLANES):
            rows = slice(tile, tile + SUBLANES)
            totals = [[[0.0, 0.0] for _ in range(RADIX)] for _ in range(aims)]
            for place in range(count):
                aim = members[start + place][0]
                at = slice(place * grid_size + tile, place * grid_size + tile + SUBLANES)
                blocks = []
                for residue in range(RADIX):
                    real, imag = (ends[residue][part][at] for part in range(2))
                    if residue:
                        cosine, sine = twist_ref[residue, 0], twist_ref[residue, 1]
                        real, imag = real * cosine - imag * sine, imag * cosine + real * sine
                    blocks.append((real, imag))
                blocks = line_transform(blocks, -1.0)
                for block, (pot_real, pot_imag) in enumerate(blocks):
                    real, imag = (held_ref[place, part, block, rows] for part in range(2))
                    totals[aim][block][0] -= real * pot_real - imag * pot_imag
                    totals[aim][block][1] -= real * pot_imag + imag * pot_real
            for aim in sorted({members[start + place][0] for place in range(count)}):
                for part in range(2):
                    found = [totals[aim][block][part][:, :width] for block in range(RADIX)]
                    found = jnp.concatenate(found, axis=1)
                    if (aim, tile) in written:
                        found = out_refs[aim][0, part, rows] + found
                    elif started:
                        found = total_refs[aim][0, part, rows] + found
                    out_refs[aim][0, part, rows] = found
                written.add((aim, tile))


def exchange(orbitals, targets, first, tables, kernels, totals=(), **options):
    grid_size, plane = targets[0].shape[2:]
    room = padded(plane // RADIX)
    given = [*orbitals, *targets, *tables, kernels, *totals]
    whole = pl.BlockSpec(memory_space=pltpu.VMEM)
    return pl.pallas_call(
        functools.partial(exchange_body, len(orbitals), len(targets), first, len(totals) > 0),
        out_shape=[pltpu.VMEM(array.shape, F32) for array in targets],
        in_specs=[whole] * len(given),
        out_specs=[whole] * len(targets),
        scratch_shapes=[
            pltpu.VMEM((RADIX // FOLD, 2, SUBLANES * grid_size, room), F32),
            pltpu.VMEM((BATCH, 2, RADIX, grid_size, room), F32),
        ],
        compiler_params=pltpu.CompilerParams(vmem_limit_bytes=SCOPED_BYTES),
        **options,
    )(*given)


def shards(targets, occupied, kernels, partner, kernel_index):
    groups = lax.axis_size("ka")
    band_count = lax.axis_size("band")
    chips = band_count // 2

    def along(array, by):
        return lax.ppermute(array, "band", [(i, i ^ by) for i in range(band_count)])

    near_steps = list(range(chips - 2, 0, -1))
    steps = [0, chips - 1] * (BATCH // 2) + near_steps
    steps += [0] * (-len(steps) % BATCH)
    tables = [jnp.asarray(table(targets.shape[2])) for table in (plane_tables, twist_tables)]
    kernel_blocks, shift, own, target, *tables = prepare(
        steps, partner, kernel_index, kernels, occupied, targets, *tables
    )
    shifts = list(range(groups - 1, 0, -1))
    came = [lax.ppermute(occupied, "ka", [(i ^ by, i) for i in range(groups)]) for by in shifts]
    visitor = choose(shift, [0, *shifts], [own, *came])

    sibling = along(target, 1)
    early = [visitor, along(visitor, 2 * (chips - 1))]
    late = [along(visitor, 2 * step) for step in near_steps]
    free = pl.CostEstimate(flops=0, bytes_accessed=0, transcendentals=0)
    mine, other = exchange(early, [target, sibling], 0, tables, kernel_blocks, cost_estimate=free)
    (other,) = exchange(late, [sibling], 1, tables, kernel_blocks, [other])
    came = along(other, 1)
    (mine,) = exchange(late, [target], 1, tables, kernel_blocks, [mine])
    return mine + came


def solution(mesh):
    return jax.shard_map(
        shards,
        mesh=mesh,
        in_specs=(
            P(("ka", "band"), None, None, None),
            P(("ka", "band"), None, None, None),
            P(),
            P(),
            P(),
        ),
        out_specs=P(("ka", "band"), None, None, None),
        check_vma=False,
    )
```

```python
import functools
import math

import jax
import jax.numpy as jnp
import ml_dtypes
import numpy as np
from jax import lax
from jax.experimental import pallas as pl
from jax.experimental.pallas import tpu as pltpu
from jax.sharding import PartitionSpec as P

KPT_DEV = 2
RADIX = 6
BATCH = 4
LANES = 128
SUBLANES = 8
FOLD = SUBLANES // BATCH
CARRIED = 4
SCOPED_BYTES = 16 * 1024 * 1024
BF16 = jnp.bfloat16
F32 = jnp.float32


def split_table(table):
    high = table.astype(ml_dtypes.bfloat16)
    low = (table - high.astype(np.float64)).astype(ml_dtypes.bfloat16)
    return high, low


def padded(width):
    return -(-width // LANES) * LANES


def plane_tables(grid_size):
    inner = grid_size // RADIX
    width = inner * grid_size
    room = padded(width) - width
    b, c = np.divmod(np.arange(width), grid_size)
    turns = RADIX * b[:, None] * b[None, :] + c[:, None] * c[None, :]
    angles = (turns % grid_size) * (2.0 * np.pi / grid_size)
    cosine = np.pad(np.cos(angles), [(0, room)] * 2)
    sine = np.pad(np.sin(angles), [(0, room)] * 2)
    found = [split_table(np.block([[cosine, -sign * sine], [sign * sine, cosine]])) for sign in (1.0, -1.0)]
    return np.array(found)


def twist_tables(grid_size):
    width = grid_size // RADIX * grid_size
    b = np.pad(np.arange(width) // grid_size, (0, padded(width) - width))
    angles = np.arange(RADIX)[:, None] * b[None, :] * (2.0 * np.pi / grid_size)
    found = np.stack([np.cos(angles), np.sin(angles)], axis=1)
    return np.repeat(found[:, :, None], SUBLANES, axis=2).astype(np.float32)


def halves(values):
    high = values.astype(BF16)
    return high, (values - high.astype(F32)).astype(BF16)


def plane_transform(real, imag, tables):
    high, low = halves(jnp.concatenate([real, imag], axis=1))
    count = high.shape[0]
    both = jnp.dot(jnp.concatenate([high, low], axis=0), tables[0], preferred_element_type=F32)
    found = both[:count] + (both[count:] + jnp.dot(high, tables[1], preferred_element_type=F32))
    half = found.shape[1] // 2
    return found[:, :half], found[:, half:]


def turn(value, angle):
    real, imag = value
    eighths = angle * 8
    if eighths == int(eighths):
        eighth = int(eighths) % 8
        if eighth % 2:
            half = math.sqrt(0.5)
            real, imag = (real + imag) * half, (imag - real) * half
        for _ in range(eighth // 2):
            real, imag = imag, -real
        return real, imag
    cosine, sine = math.cos(2 * math.pi * angle), math.sin(2 * math.pi * angle)
    return real * cosine + imag * sine, imag * cosine - real * sine


def plus(left, right):
    return left[0] + right[0], left[1] + right[1]


def minus(left, right):
    return left[0] - right[0], left[1] - right[1]


def three_points(first, second, third, sign):
    total = plus(second, third)
    apart = minus(second, third)
    factor = sign * math.sqrt(3.0) / 2.0
    turned = (apart[1] * factor, apart[0] * -factor)
    middle = (first[0] - 0.5 * total[0], first[1] - 0.5 * total[1])
    return [plus(first, total), plus(middle, turned), minus(middle, turned)]


def line_transform(values, sign):
    size = len(values)
    if size == 1:
        return values
    if size == 3:
        return three_points(*values, sign)
    odd = size
    while odd % 2 == 0:
        odd //= 2
    if odd == 1:
        even = line_transform(values[0::2], sign)
        other = line_transform(values[1::2], sign)
        other = [turn(value, sign * k / size) for k, value in enumerate(other)]
        return [plus(*both) for both in zip(even, other)] + [minus(*both) for both in zip(even, other)]
    if odd == size:
        found = []
        for k in range(size):
            total = values[0]
            for n in range(1, size):
                total = plus(total, turn(values[n], sign * (k * n % size) / size))
            found.append(total)
        return found
    twos = size // odd
    rows = []
    for i in range(odd):
        rows.append(line_transform([values[(twos * i + odd * j) % size] for j in range(twos)], sign))
    columns = [line_transform([row[j] for row in rows], sign) for j in range(twos)]
    return [columns[k % twos][k % odd] for k in range(size)]


def prepare_body(steps, partner_ref, index_ref, kernels_ref, *refs):
    carried, (out_ref, shift_ref), refs = refs[:CARRIED], refs[CARRIED : CARRIED + 2], refs[CARRIED + 2 :]
    copied, (partner, index, held, sems) = refs[:CARRIED], refs[CARRIED:]
    copies = []
    moves = [(partner_ref, partner), (index_ref, index), (kernels_ref, held), *zip(carried, copied)]
    for number, (source, target) in enumerate(moves):
        copy = pltpu.make_async_copy(source, target, sems.at[number])
        copy.start()
        copies.append(copy)
    group = lax.axis_index("ka")
    position = lax.axis_index("band")
    per_kpoint = lax.axis_size("band") // KPT_DEV
    kpoint = group * KPT_DEV + position // per_kpoint
    grid_size = kernels_ref.shape[1]
    inner = grid_size // RADIX
    width = inner * grid_size
    slots = lax.broadcasted_iota(jnp.int32, (SUBLANES, LANES), 0)
    chosen = []
    for start in range(0, len(steps), BATCH):
        local_of = jnp.zeros((SUBLANES, LANES), jnp.int32)
        for slot, step in enumerate(steps[start : start + BATCH] * FOLD):
            local = (position ^ (2 * step)) // per_kpoint
            local_of = jnp.where(slots == slot, local, local_of)
        chosen.append([local_of == local for local in range(KPT_DEV)])
    for copy in copies[:3]:
        copy.wait()
    shift_ref[0] = partner[group] ^ group
    numbers = [index[kpoint, partner[group] * KPT_DEV + local] for local in range(KPT_DEV)]
    scale = 1.0 / grid_size**3
    room = jnp.zeros((grid_size, padded(width) - width), F32)
    for residue in range(RADIX):
        fold, upper = divmod(residue, FOLD)
        arranged = []
        for number in numbers:
            blocks = []
            for q in range(inner):
                at = (RADIX * q + residue) * grid_size
                blocks.append(held[number, :, at : at + grid_size])
            arranged.append(jnp.concatenate([*blocks, room], axis=1) * scale)
        rows = slice(upper * BATCH, (upper + 1) * BATCH)
        for lane in range(padded(width) // LANES):
            at = slice(lane * LANES, (lane + 1) * LANES)
            for p in range(grid_size):
                values = [jnp.broadcast_to(value[p : p + 1, at], (SUBLANES, LANES)) for value in arranged]
                for batch, masks in enumerate(chosen):
                    found = values[0]
                    for local in range(1, KPT_DEV):
                        found = jnp.where(masks[local], values[local], found)
                    out_ref[batch, fold, lane, p, rows] = found[rows]
    for copy in copies[3:]:
        copy.wait()


def in_hbm(array):
    return pltpu.with_memory_space_constraint(array, pltpu.HBM)


def prepare(steps, partner, kernel_index, kernels, *carried):
    grid_size, plane = kernels.shape[1:]
    batches = len(steps) // BATCH
    lanes = padded(plane // RADIX) // LANES
    given = [partner, kernel_index, kernels, *carried]
    return pl.pallas_call(
        functools.partial(prepare_body, steps),
        out_shape=[
            pltpu.VMEM((batches, RADIX // FOLD, lanes, grid_size, SUBLANES, LANES), F32),
            pltpu.SMEM((1,), jnp.int32),
            *[pltpu.VMEM(array.shape, array.dtype) for array in carried],
        ],
        in_specs=[pl.BlockSpec(memory_space=pltpu.HBM)] * len(given),
        out_specs=[
            pl.BlockSpec(memory_space=pltpu.VMEM),
            pl.BlockSpec(memory_space=pltpu.SMEM),
            *[pl.BlockSpec(memory_space=pltpu.VMEM)] * len(carried),
        ],
        scratch_shapes=[
            pltpu.SMEM(partner.shape, jnp.int32),
            pltpu.SMEM(kernel_index.shape, jnp.int32),
            pltpu.VMEM(kernels.shape, F32),
            pltpu.SemaphoreType.DMA((len(given),)),
        ],
        compiler_params=pltpu.CompilerParams(vmem_limit_bytes=SCOPED_BYTES),
    )(*[in_hbm(array) for array in given])


def choose_body(shifts, shift_ref, *refs):
    for by, ref in zip(shifts, refs[:-1]):

        @pl.when(shift_ref[0] == by)
        def _(ref=ref):
            refs[-1][...] = ref[...]


def choose(shift, shifts, arrays):
    whole = pl.BlockSpec(memory_space=pltpu.VMEM)
    return pl.pallas_call(
        functools.partial(choose_body, shifts),
        out_shape=pltpu.VMEM(arrays[0].shape, arrays[0].dtype),
        in_specs=[pl.BlockSpec(memory_space=pltpu.SMEM), *[whole] * len(arrays)],
        out_specs=whole,
        compiler_params=pltpu.CompilerParams(vmem_limit_bytes=SCOPED_BYTES),
    )(shift, *arrays)


def lane_blocks(values, width):
    rows, plane = values.shape
    found = []
    for block in range(RADIX):
        at, room = block * width, padded(width)
        if at + room <= plane:
            found.append(values[:, at : at + room])
        else:
            blank = jnp.zeros((rows, at + room - plane), values.dtype)
            found.append(jnp.concatenate([values[:, at:], blank], axis=1))
    return found


def exchange_body(given, aims, first, started, *refs):
    orbital_refs, target_refs, refs = refs[:given], refs[given : given + aims], refs[given + aims :]
    plane_ref, twist_ref, kernel_ref, refs = refs[0], refs[1], refs[2], refs[3:]
    total_refs, refs = refs[: aims * started], refs[aims * started :]
    out_refs, (field_ref, held_ref) = refs[:aims], refs[aims:]
    grid_size, plane = target_refs[0].shape[2:]
    width = plane // RADIX
    lanes = padded(width) // LANES
    members = [(aim, ref, row) for aim in range(aims) for ref in orbital_refs for row in range(ref.shape[0])]
    written = set()
    for start in range(0, len(members), BATCH):
        batch = first + start // BATCH
        count = min(BATCH, len(members) - start)
        size = count * grid_size
        for place, (_, ref, row) in enumerate(members[start : start + count]):
            for part in range(2):
                for block, values in enumerate(lane_blocks(ref[row, part], width)):
                    held_ref[place, part, block] = values.astype(F32)
        starts = {}
        for tile in range(0, grid_size, SUBLANES):
            rows = slice(tile, tile + SUBLANES)
            targets = [[lane_blocks(ref[0, part, rows], width) for part in range(2)] for ref in target_refs]
            for place in range(count):
                blocks = []
                for block in range(RADIX):
                    real, imag = (held_ref[place, part, block, rows] for part in range(2))
                    target_real, target_imag = (targets[members[start + place][0]][part][block] for part in range(2))
                    blocks.append(
                        (
                            real * target_real + imag * target_imag,
                            real * target_imag - imag * target_real,
                        )
                    )
                at = place * grid_size + tile
                for residue, (real, imag) in enumerate(line_transform(blocks, 1.0)):
                    if residue:
                        cosine, sine = twist_ref[residue, 0], twist_ref[residue, 1]
                        real, imag = real * cosine + imag * sine, imag * cosine - real * sine
                    starts[residue, 0, at], starts[residue, 1, at] = real, imag

        def over_plane(fold):
            residues = range(fold * FOLD, (fold + 1) * FOLD)
            places = [(residue, at) for residue in residues for at in range(0, size, SUBLANES)]
            parts = [jnp.concatenate([starts[residue, part, at] for residue, at in places], axis=0) for part in range(2)]
            parts = plane_transform(*parts, [plane_ref[0, j] for j in range(2)])
            for part in range(2):
                for upper in range(FOLD):
                    at = upper * BATCH * grid_size
                    field_ref[fold, part, at : at + size] = parts[part][upper * size : (upper + 1) * size]

        def over_line(fold):
            for lane in range(lanes):
                at = slice(lane * LANES, (lane + 1) * LANES)
                values = [
                    tuple(field_ref[fold, part, pl.ds(a, SUBLANES, stride=grid_size), at] for part in range(2))
                    for a in range(grid_size)
                ]
                scaled = []
                for p, (real, imag) in enumerate(line_transform(values, 1.0)):
                    kernel = kernel_ref[batch, fold, lane, p]
                    scaled.append((real * kernel, imag * kernel))
                for a, value in enumerate(line_transform(scaled, -1.0)):
                    for part in range(2):
                        field_ref[fold, part, pl.ds(a, SUBLANES, stride=grid_size), at] = value[part]

        ends = {}

        def back(fold):
            parts = []
            for part in range(2):
                at = [upper * BATCH * grid_size for upper in range(FOLD)]
                parts.append(jnp.concatenate([field_ref[fold, part, start : start + size] for start in at], axis=0))
            parts = plane_transform(*parts, [plane_ref[1, j] for j in range(2)])
            for upper in range(FOLD):
                ends[fold * FOLD + upper] = [values[upper * size : (upper + 1) * size] for values in parts]

        folds = RADIX // FOLD
        for turn_number in range(folds + 2):
            if turn_number < folds:
                over_plane(turn_number)
            if 0 <= turn_number - 1 < folds:
                over_line(turn_number - 1)
            if 0 <= turn_number - 2 < folds:
                back(turn_number - 2)
        for tile in range(0, grid_size, SUBLANES):
            rows = slice(tile, tile + SUBLANES)
            totals = [[[0.0, 0.0] for _ in range(RADIX)] for _ in range(aims)]
            for place in range(count):
                aim = members[start + place][0]
                at = slice(place * grid_size + tile, place * grid_size + tile + SUBLANES)
                blocks = []
                for residue in range(RADIX):
                    real, imag = (ends[residue][part][at] for part in range(2))
                    if residue:
                        cosine, sine = twist_ref[residue, 0], twist_ref[residue, 1]
                        real, imag = real * cosine - imag * sine, imag * cosine + real * sine
                    blocks.append((real, imag))
                blocks = line_transform(blocks, -1.0)
                for block, (pot_real, pot_imag) in enumerate(blocks):
                    real, imag = (held_ref[place, part, block, rows] for part in range(2))
                    totals[aim][block][0] -= real * pot_real - imag * pot_imag
                    totals[aim][block][1] -= real * pot_imag + imag * pot_real
            for aim in sorted({members[start + place][0] for place in range(count)}):
                for part in range(2):
                    found = [totals[aim][block][part][:, :width] for block in range(RADIX)]
                    found = jnp.concatenate(found, axis=1)
                    if (aim, tile) in written:
                        found = out_refs[aim][0, part, rows] + found
                    elif started:
                        found = total_refs[aim][0, part, rows] + found
                    out_refs[aim][0, part, rows] = found
                written.add((aim, tile))


def exchange(orbitals, targets, first, tables, kernels, totals=(), **options):
    grid_size, plane = targets[0].shape[2:]
    room = padded(plane // RADIX)
    given = [*orbitals, *targets, *tables, kernels, *totals]
    whole = pl.BlockSpec(memory_space=pltpu.VMEM)
    return pl.pallas_call(
        functools.partial(exchange_body, len(orbitals), len(targets), first, len(totals) > 0),
        out_shape=[pltpu.VMEM(array.shape, F32) for array in targets],
        in_specs=[whole] * len(given),
        out_specs=[whole] * len(targets),
        scratch_shapes=[
            pltpu.VMEM((RADIX // FOLD, 2, SUBLANES * grid_size, room), F32),
            pltpu.VMEM((BATCH, 2, RADIX, grid_size, room), F32),
        ],
        compiler_params=pltpu.CompilerParams(vmem_limit_bytes=SCOPED_BYTES),
        **options,
    )(*given)


def shards(targets, occupied, kernels, partner, kernel_index):
    groups = lax.axis_size("ka")
    band_count = lax.axis_size("band")
    chips = band_count // 2

    def along(array, by):
        return lax.ppermute(array, "band", [(i, i ^ by) for i in range(band_count)])

    near_steps = list(range(chips - 2, 0, -1))
    steps = [0, chips - 1] * (BATCH // 2) + near_steps
    steps += [0] * (-len(steps) % BATCH)
    tables = [jnp.asarray(table(targets.shape[2])) for table in (plane_tables, twist_tables)]
    kernel_blocks, shift, own, target, *tables = prepare(
        steps, partner, kernel_index, kernels, occupied, targets, *tables
    )
    shifts = list(range(groups - 1, 0, -1))
    came = [lax.ppermute(occupied, "ka", [(i ^ by, i) for i in range(groups)]) for by in shifts]
    visitor = choose(shift, [0, *shifts], [own, *came])

    sibling = along(targets, 1)
    early = [visitor, along(visitor, 2 * (chips - 1))]
    late = [along(visitor, 2 * step) for step in near_steps]
    free = pl.CostEstimate(flops=0, bytes_accessed=0, transcendentals=0)
    mine, other = exchange(early, [target, sibling], 0, tables, kernel_blocks, cost_estimate=free)
    (other,) = exchange(late, [sibling], 1, tables, kernel_blocks, [other])
    came = along(other, 1)
    (mine,) = exchange(late, [target], 1, tables, kernel_blocks, [mine])
    return mine + came


def solution(mesh):
    return jax.shard_map(
        shards,
        mesh=mesh,
        in_specs=(
            P(("ka", "band"), None, None, None),
            P(("ka", "band"), None, None, None),
            P(),
            P(),
            P(),
        ),
        out_specs=P(("ka", "band"), None, None, None),
        check_vma=False,
    )
```
